32 devices in a mesh: rows: 8 (over z, x), seq: 4 (over y, core).
Axes of the slice: x: 2, y: 2, z: 4, core: 2. Of those that a mesh axis runs over, the one named last changes fastest.
Arguments:
- layer_input: float32 [8, 1024, 768], P('rows', 'seq'), may hold values from -6 to 6
- doc_lengths: int32 [8, 4], P('rows'), may hold values from 1 to 976, as said below
- output_grad: float32 [8, 1024, 768], P('rows', 'seq'), may hold values from -6 to 6
- mixer_gain: float32 [768], replicated, may hold values from 0.5 to 1.5
- triple_weight: float32 [768, 2304], replicated, may hold values from -0.21875 to 0.21875
- rate_weight: float32 [768, 12], replicated, may hold values from -0.21875 to 0.21875
- rate_bias: float32 [12], replicated, may hold values from -3 to 3
- first_weight: float32 [12, 64, 256], replicated, may hold values from -0.75 to 0.75
- first_bias: float32 [12, 256], replicated, may hold values from -3 to 3
- second_weight: float32 [12, 256, 64], replicated, may hold values from -0.375 to 0.375
- second_bias: float32 [12, 64], replicated, may hold values from -3 to 3
- inner_gain: float32 [12, 64], replicated, may hold values from 0.5 to 1.5
- inner_shift: float32 [12, 64], replicated, may hold values from -3 to 3
- gate_weight: float32 [768, 768], replicated, may hold values from -0.21875 to 0.21875
- output_weight: float32 [768, 768], replicated, may hold values from -0.21875 to 0.21875
- feed_gain: float32 [768], replicated, may hold values from 0.5 to 1.5
- feed_weight: float32 [768, 4096], replicated, may hold values from -0.21875 to 0.21875
- down_weight: float32 [2048, 768], replicated, may hold values from -0.125 to 0.125
Outputs:
- layer_output: float32 [8, 1024, 768], P('rows', 'seq')
- input_grad: float32 [8, 1024, 768], P('rows', 'seq')
- mixer_gain_grad: float32 [768], replicated
- triple_weight_grad: float32 [768, 2304], P('rows', 'seq')
- rate_weight_grad: float32 [768, 12], replicated
- rate_bias_grad: float32 [12], replicated
- first_weight_grad: float32 [12, 64, 256], replicated
- first_bias_grad: float32 [12, 256], replicated
- second_weight_grad: float32 [12, 256, 64], replicated
- second_bias_grad: float32 [12, 64], replicated
- inner_gain_grad: float32 [12, 64], replicated
- inner_shift_grad: float32 [12, 64], replicated
- gate_weight_grad: float32 [768, 768], P('rows', 'seq')
- output_weight_grad: float32 [768, 768], P('rows', 'seq')
- feed_gain_grad: float32 [768], replicated
- feed_weight_grad: float32 [768, 4096], P('rows', 'seq')
- down_weight_grad: float32 [2048, 768], P('rows', 'seq')
The draws below stay inside these ranges and needn't reach their ends.
Inputs may be any that keep to these rules, and one draw needn't show every extreme that they name: `doc_lengths`: each row holds 4 documents in order, each starting on a multiple of 16 tokens and taking ceil(length / 16) whole mini-batches; together they take exactly the row's 1024 / 16 mini-batches. The second document of every row starts in the row's first 256 tokens and ends in its last 256.
All inputs are finite; a program needn't handle non-finite values.
Results may differ from the reference program's by a relative error of at most 0.0003.
Values sent between devices are 32-bit elements; how exact they have to be, the bound alone decides.
No kernel may reach another device: no remote copies, remote signals or barrier semaphores. Data moves between devices by JAX's collectives and lax.ppermute only.
A program may use at most 256 MiB of HBM per device.

```python
import jax
import jax.numpy as jnp
from jax import lax

D = 768
HEADS = 12
HEAD = 64
INNER = 256
FF = 2048
MB = 16
NDOC = 4
GROUP = 256
SEQ_LEN = 1024
ROWS = 8


def draw_doc_lengths(key, part):
    key = jax.random.fold_in(key, 11)
    total_blocks = SEQ_LEN // MB
    group_blocks = GROUP // MB
    subkeys = jax.random.split(key, 3)
    first_row = jnp.arange(ROWS, dtype=jnp.int32)[:, None] == 0
    opening = jax.random.randint(subkeys[0], (ROWS, 1), 1, group_blocks // 2 + 1)
    opening = jnp.where(first_row, 1, opening)
    others = jax.random.randint(subkeys[1], (ROWS, NDOC - 2), 1, max((group_blocks - 1) // (NDOC - 2), 1) + 1)
    others = jnp.where(first_row, 1, others)
    longest = total_blocks - opening - jnp.sum(others, axis=1, keepdims=True)
    block_counts = jnp.concatenate([opening, longest, others], axis=1)
    shortfall = jax.random.randint(subkeys[2], (ROWS, NDOC), 0, MB)
    column = jnp.arange(NDOC, dtype=jnp.int32)[None, :]
    shortfall = jnp.where(first_row & (column == 0), MB - 1, shortfall)
    shortfall = jnp.where(first_row & (column == 1), 0, shortfall)
    return (block_counts * MB - shortfall).astype(jnp.int32)


def block_scale(own_key, dims, pieces, low, top_value):
    def one(axis_at, shards_of):
        steps = jax.random.uniform(jax.random.fold_in(jax.random.fold_in(own_key, 6), axis_at), (shards_of,), jnp.float32, low / len(pieces), top_value / len(pieces))
        return jnp.repeat(jnp.exp(steps), dims[axis_at] // shards_of).reshape((-1,) + (1,) * (len(dims) - axis_at - 1))

    loudness = one(*pieces[0])
    for cut in pieces[1:]:
        loudness = loudness * one(*cut)
    return loudness


def centred(key, shape, scale, limit, cuts=(), kind=jnp.bfloat16):
    level = block_scale(key, shape, cuts, -0.22, 0.18) if cuts else 1.0
    entries = jax.random.normal(key, shape, jnp.float32) * scale * level
    return jnp.minimum(jnp.maximum(entries, -limit), limit).astype(kind)


def setup_inputs(seed: int = 0) -> dict:
    streams_of = jax.random.split(jax.random.key(seed), 19)
    layer_input = centred(streams_of[0], (ROWS, SEQ_LEN, D), 1.0, 6.0, ((0, 8), (1, 4)), jnp.float32)
    doc_lengths = draw_doc_lengths(jax.random.fold_in(streams_of[18], 71), 0)
    output_grad = centred(streams_of[2], (ROWS, SEQ_LEN, D), 1.0, 6.0, ((0, 8), (1, 4)), jnp.float32)
    mixer_gain = jnp.clip(1.0 + 0.1 * jax.random.normal(streams_of[3], (D,), jnp.float32), 0.5, 1.5)
    triple_weight = centred(streams_of[4], (D, 3 * D), D ** -0.5, 0.21875, (), jnp.float32)
    rate_weight = centred(streams_of[5], (D, HEADS), D ** -0.5, 0.21875, (), jnp.float32)
    rate_bias = centred(streams_of[6], (HEADS,), 1.0, 3.0, (), jnp.float32)
    first_weight = centred(streams_of[7], (HEADS, HEAD, INNER), HEAD ** -0.5, 0.75, (), jnp.float32)
    first_bias = centred(streams_of[8], (HEADS, INNER), 0.5, 3.0, (), jnp.float32)
    second_weight = centred(streams_of[9], (HEADS, INNER, HEAD), INNER ** -0.5, 0.375, (), jnp.float32)
    second_bias = centred(streams_of[10], (HEADS, HEAD), 0.5, 3.0, (), jnp.float32)
    inner_gain = jnp.clip(1.0 + 0.1 * jax.random.normal(streams_of[11], (HEADS, HEAD), jnp.float32), 0.5, 1.5)
    inner_shift = centred(streams_of[12], (HEADS, HEAD), 0.5, 3.0, (), jnp.float32)
    gate_weight = centred(streams_of[13], (D, D), D ** -0.5, 0.21875, (), jnp.float32)
    output_weight = centred(streams_of[14], (D, D), D ** -0.5, 0.21875, (), jnp.float32)
    feed_gain = jnp.clip(1.0 + 0.1 * jax.random.normal(streams_of[15], (D,), jnp.float32), 0.5, 1.5)
    feed_weight = centred(streams_of[16], (D, 2 * FF), D ** -0.5, 0.21875, (), jnp.float32)
    down_weight = centred(streams_of[17], (FF, D), FF ** -0.5, 0.125, (), jnp.float32)
    return {"layer_input": layer_input, "doc_lengths": doc_lengths, "output_grad": output_grad, "mixer_gain": mixer_gain, "triple_weight": triple_weight, "rate_weight": rate_weight, "rate_bias": rate_bias, "first_weight": first_weight, "first_bias": first_bias, "second_weight": second_weight, "second_bias": second_bias, "inner_gain": inner_gain, "inner_shift": inner_shift, "gate_weight": gate_weight, "output_weight": output_weight, "feed_gain": feed_gain, "feed_weight": feed_weight, "down_weight": down_weight}


highest = lax.Precision.HIGHEST
base_rate = 0.1
epsilon = 1e-06
root_two_pi = 0.7978845608028654

@jax.custom_vjp
def low(v):
    return lax.optimization_barrier(v.astype(jnp.bfloat16)).astype(jnp.float32)

@jax.custom_vjp
def low_back(v):
    return v

def low_keep(v):
    return (low(v), None)

def low_pass(kept, grad):
    return (grad,)

def back_keep(v):
    return (v, None)

def back_low(kept, grad):
    return (low(grad),)
low.defvjp(low_keep, low_pass)
low_back.defvjp(back_keep, back_low)

def gelu_tanh(value_in):
    cubic = root_two_pi * (value_in + 0.044715 * value_in * value_in * value_in)
    return 0.5 * value_in * (1.0 + jnp.tanh(cubic))

def gelu_slope(value_in):
    tangent = jnp.tanh(root_two_pi * (value_in + 0.044715 * value_in * value_in * value_in))
    return 0.5 * (1.0 + tangent) + 0.5 * value_in * (1.0 - tangent * tangent) * root_two_pi * (1.0 + 0.134145 * value_in * value_in)

def rms_scale(value_in, norm_gain):
    return value_in * lax.rsqrt(lax.optimization_barrier(jnp.mean(value_in * value_in, axis=-1, keepdims=True)) + epsilon) * norm_gain

def layer_norm(value_in):
    centered = value_in - lax.optimization_barrier(jnp.mean(value_in, axis=-1, keepdims=True))
    inverse = lax.rsqrt(lax.optimization_barrier(jnp.mean(centered * centered, axis=-1, keepdims=True)) + epsilon)
    return (centered * inverse, inverse)

def inner_step(carried, minibatch, initial, norm_pair):
    query_heads, key_heads, value_heads, rate_vals, reset_flag = minibatch
    carried = tuple((reset_flag * learned + (1.0 - reset_flag) * current for learned, current in zip(initial, carried)))
    weight_in, bias_in, weight_out, bias_out = carried
    norm_gain = norm_pair[0][:, None, :]
    norm_shift = norm_pair[1][:, None, :]
    pre_hidden = jnp.einsum('htk,hki->hti', key_heads, weight_in, precision=highest) + bias_in[:, None, :]
    activated = gelu_tanh(pre_hidden)
    pre_out = jnp.einsum('hti,hik->htk', activated, weight_out, precision=highest) + bias_out[:, None, :]
    normed, inverse = layer_norm(pre_out)
    target = value_heads - key_heads
    scaled = (norm_gain * normed + norm_shift - target) * norm_gain
    out_grad = inverse * (scaled - lax.optimization_barrier(jnp.mean(scaled, axis=-1, keepdims=True)) - normed * lax.optimization_barrier(jnp.mean(scaled * normed, axis=-1, keepdims=True)))
    hidden_grad = jnp.einsum('htk,hik->hti', out_grad, weight_out, precision=highest) * gelu_slope(pre_hidden)
    length = query_heads.shape[1]
    causal = jnp.tril(jnp.ones((length, length), jnp.float32))
    step_rates = causal[None, :, :] * rate_vals[:, None, :]
    query_key = jnp.einsum('htk,hsk->hts', query_heads, key_heads, precision=highest) + 1.0
    query_pre = jnp.einsum('htk,hki->hti', query_heads, weight_in, precision=highest) + bias_in[:, None, :] - jnp.einsum('hts,hsi->hti', step_rates * query_key, hidden_grad, precision=highest)
    query_act = gelu_tanh(query_pre)
    query_act_key = jnp.einsum('hti,hsi->hts', query_act, activated, precision=highest) + 1.0
    query_out = jnp.einsum('hti,hik->htk', query_act, weight_out, precision=highest) + bias_out[:, None, :] - jnp.einsum('hts,hsk->htk', step_rates * query_act_key, out_grad, precision=highest)
    query_norm = layer_norm(query_out)[0]
    result = query_heads + norm_gain * query_norm + norm_shift
    rated_hidden = rate_vals[:, :, None] * hidden_grad
    rated_out = rate_vals[:, :, None] * out_grad
    updated = (weight_in - jnp.einsum('htk,hti->hki', key_heads, rated_hidden, precision=highest), bias_in - lax.optimization_barrier(jnp.sum(rated_hidden, axis=1)), weight_out - jnp.einsum('hti,htk->hik', activated, rated_out, precision=highest), bias_out - lax.optimization_barrier(jnp.sum(rated_out, axis=1)))
    return (updated, result)

def doc_masks(lengths, offset, span):
    block_counts = (lengths + MB - 1) // MB
    begins = jnp.cumsum(block_counts, dtype=jnp.int32) - block_counts
    block_index = offset // MB + jnp.arange(span // MB, dtype=jnp.int32)
    resets = jnp.any(block_index[:, None] == begins[None, :], axis=1).astype(jnp.float32)
    positions = offset + jnp.arange(span, dtype=jnp.int32)
    starts = begins * MB
    inside = (positions[:, None] >= starts[None, :]) & (positions[:, None] < (starts + lengths)[None, :])
    return (resets, jnp.any(inside, axis=1).astype(jnp.float32))

def forward_row(params, row_input, resets, valid_mask):
    mixer_gain, triple_weight, rate_weight, rate_bias, first_weight, first_bias, second_weight, second_bias, inner_gain, inner_shift, gate_weight, output_weight, feed_gain, feed_weight, down_weight = params
    block_total = SEQ_LEN // MB
    normed = rms_scale(row_input, mixer_gain)
    triple = jnp.dot(normed, triple_weight, precision=highest)

    def arrange(columns):
        return columns.reshape(block_total, MB, HEADS, HEAD).transpose(0, 2, 1, 3)
    rate_vals = base_rate / HEAD * jax.nn.sigmoid(jnp.dot(normed, rate_weight, precision=highest) + rate_bias) * valid_mask[:, None]
    rate_vals = rate_vals.reshape(block_total, MB, HEADS).transpose(0, 2, 1)
    initial = (first_weight, first_bias, second_weight, second_bias)
    norm_pair = (inner_gain, inner_shift)

    def step(carried, minibatch):
        return inner_step(carried, minibatch, initial, norm_pair)
    features = (arrange(triple[:, :D]), arrange(triple[:, D:2 * D]), arrange(triple[:, 2 * D:]), rate_vals, resets)
    final_state, results = lax.scan(jax.checkpoint(step), initial, features)
    mixed_heads = results.transpose(0, 2, 1, 3).reshape(SEQ_LEN, D)
    gated_mix = gelu_tanh(jnp.dot(normed, gate_weight, precision=highest)) * mixed_heads
    middle = row_input + jnp.dot(gated_mix, output_weight, precision=highest)
    second = rms_scale(middle, feed_gain)
    both = jnp.dot(second, feed_weight, precision=highest)
    hidden = jax.nn.silu(both[:, :FF]) * both[:, FF:]
    return middle + jnp.dot(hidden, down_weight, precision=highest)

def add_up(left, right):
    return left + right

def reference(layer_input, doc_lengths, output_grad, mixer_gain, triple_weight, rate_weight, rate_bias, first_weight, first_bias, second_weight, second_bias, inner_gain, inner_shift, gate_weight, output_weight, feed_gain, feed_weight, down_weight):
    params = (mixer_gain, triple_weight, rate_weight, rate_bias, first_weight, first_bias, second_weight, second_bias, inner_gain, inner_shift, gate_weight, output_weight, feed_gain, feed_weight, down_weight)

    def one_row(running, row_data):
        row_input, lengths, cotangent = row_data
        resets, valid_mask = doc_masks(lengths, 0, SEQ_LEN)

        def forward(weights, inputs):
            return forward_row(weights, inputs, resets, valid_mask)
        row_output, pullback = jax.vjp(forward, params, row_input)
        weight_grads, input_part = pullback(cotangent)
        running = jax.tree.map(add_up, running, weight_grads)
        return (running, (row_output, input_part))
    zero_grads = jax.tree.map(jnp.zeros_like, params)
    totals, outputs = lax.scan(one_row, zero_grads, (layer_input, doc_lengths, output_grad))
    return (outputs[0], outputs[1], totals[0], totals[1], totals[2], totals[3], totals[4], totals[5], totals[6], totals[7], totals[8], totals[9], totals[10], totals[11], totals[12], totals[13], totals[14])
```

```python
import functools
import jax
import jax.numpy as jnp
from jax import lax
from jax.experimental import pallas as pl
from jax.experimental.pallas import tpu as pltpu
from jax.sharding import PartitionSpec as P

HEAD = 64
INNER = 256
MB = 16
EPS = 1e-06
RTP = 0.7978845608028654
F32 = jnp.float32
BF16 = jnp.bfloat16
LANES = 128


def hi_lo(value):
    high = value.astype(BF16)
    return high, (value - high.astype(F32)).astype(BF16)


def mm(left, right):
    return lax.dot_general(left, right, (((1,), (0,)), ((), ())), preferred_element_type=F32)


def mm_nt(left, right):
    return lax.dot_general(left, right, (((1,), (1,)), ((), ())), preferred_element_type=F32)


def mm_tn(left, right):
    return lax.dot_general(left, right, (((0,), (0,)), ((), ())), preferred_element_type=F32)


def rows2(*parts):
    return jnp.concatenate(parts, axis=0)


def fold(value):
    return value[:MB] + value[MB:]


def half_turn(value):
    return pltpu.roll(value, HEAD, 1)


def both_halves(value):
    return value + half_turn(value)


def lane_of(shape):
    return lax.broadcasted_iota(jnp.int32, shape, 1)


def pick(block, unit):
    tile = block[:, (unit // 2) * LANES : (unit // 2 + 1) * LANES]
    turned = half_turn(tile)
    low_half = lane_of(tile.shape) < HEAD
    if unit % 2 == 0:
        return jnp.where(low_half, tile, turned)
    return jnp.where(low_half, turned, tile)


def pack(parts):
    tiles = []
    for at in range(0, len(parts), 2):
        left = parts[at]
        right = parts[at + 1] if at + 1 < len(parts) else jnp.zeros_like(left)
        tiles.append(jnp.where(lane_of(left.shape) < HEAD, left, right))
    return jnp.concatenate(tiles, axis=1) if len(tiles) > 1 else tiles[0]


def mean_dup(value):
    return jnp.sum(value, axis=1, keepdims=True) * (1.0 / LANES)


def gelu_parts(z):
    z2 = z * z
    t = jnp.tanh(z * (RTP + (RTP * 0.044715) * z2))
    one_t = 0.5 + 0.5 * t
    sech = (1.0 - t) * one_t
    inner = RTP + (RTP * 0.134145) * z2
    act = z * one_t
    zs = z * sech
    slope = one_t + zs * inner
    return act, slope, t, zs, sech, inner


def gelu_curve(z, t, zs, sech, inner):
    return 2.0 * sech * inner + zs * ((2.0 * RTP * 0.134145) * z) - 2.0 * t * zs * inner * inner


def split3(high, low):
    return rows2(high, high, low)


def stack3(high, low):
    return rows2(high, low, high)


def lanes3(value):
    high, low = hi_lo(value)
    lane = lane_of(value.shape)
    return jnp.where((lane >= MB) & (lane < 2 * MB), low.astype(F32), high.astype(F32)).astype(BF16)


def fwd_kernel(heads, steps, resets_ref, qkv_ref, rate_ref, gain_ref, shift_ref, w1i, b1i, w2i, b2i,
               out_ref, s1_ref, s2_ref, z1_ref, zq_ref, m_ref, d2_ref, x_ref, y_ref, r_ref, rq_ref,
               w1, b1, w2, b2):
    block = pl.program_id(0)

    def step(i, carry):
        at = block * steps + i

        @pl.when(resets_ref[at] == 1)
        def _():
            w1[...] = w1i[...]
            b1[...] = b1i[...]
            w2[...] = w2i[...]
            b2[...] = b2i[...]

        rows = pl.ds(pl.multiple_of(i * MB, MB), MB)
        qkv = qkv_ref[rows, :]
        rates = rate_ref[rows, :]
        lane = lane_of((MB, LANES))
        row = lax.broadcasted_iota(jnp.int32, (MB, LANES), 0)
        outs = []
        for h in range(heads):
            gain = gain_ref[h]
            shift = shift_ref[h]
            q = pick(qkv, h)
            k = pick(qkv, heads + h)
            v = pick(qkv, 2 * heads + h)
            e = jnp.broadcast_to(rates[:, h : h + 1], (MB, LANES))
            coef = gain * (shift - v + k)
            coef_mean = mean_dup(coef)
            gain2 = gain * gain
            khi, klo = hi_lo(k)
            qhi, qlo = hi_lo(q)
            left_a = rows2(khi, klo, qhi, qlo)
            qsplit = jnp.where(lane < HEAD, qhi.astype(F32), qlo.astype(F32)).astype(BF16)
            zero = jnp.zeros((HEAD, LANES), BF16)
            kq = fold(mm_nt(rows2(khi, klo), rows2(zero, qsplit, zero[: HEAD - MB])))
            causal = (lane >= HEAD) & (lane < HEAD + MB) & (row <= lane - HEAD)
            left_d = e * jnp.where(lane < HEAD, k, jnp.where(causal, kq + 1.0, jnp.where((lane >= HEAD + MB) & (lane < HEAD + 2 * MB), 1.0, 0.0)))
            left_d3 = jnp.transpose(stack3(*hi_lo(left_d)))[: HEAD + 2 * MB]
            erow = jnp.transpose(e)[:MB, :]
            erow3 = jnp.concatenate([erow, erow, erow], axis=1)
            lane48 = lane_of((MB, 3 * MB))
            row48 = lax.broadcasted_iota(jnp.int32, (MB, 3 * MB), 0)
            e3 = jnp.where(lax.rem(lane48, MB) <= row48, erow3, 0.0)

            w1f = w1[h]
            w2f = w2[h]
            w1s = rows2(*hi_lo(w1f))
            w2s = rows2(*hi_lo(w2f))
            s1_ref[i, h] = w1s
            s2_ref[i, h] = w2s
            b1v = b1[h]
            b2v = b2[h]
            z = mm(left_a, w1s)
            z1 = z[:MB] + z[MB : 2 * MB] + b1v
            act, slope = gelu_parts(z1)[:2]
            ahi, alo = hi_lo(act)
            left_b = rows2(ahi, alo)
            z2 = both_halves(fold(mm_nt(left_b, w2s))) + b2v
            g2z = gain2 * z2
            inv = lax.rsqrt(mean_dup(z2 * z2) + EPS)
            m1 = mean_dup(g2z)
            m2 = mean_dup(g2z * z2)
            m3 = mean_dup(coef * z2)
            x = z2 * inv
            g = gain2 * x + coef
            d2 = inv * (g - (inv * m1 + coef_mean) - x * (inv * inv * m2 + inv * m3))
            d2hi, d2lo = hi_lo(d2)
            m = fold(mm(rows2(d2hi, d2lo), w2s))
            d1 = m * slope
            u = mm(left_d3, split3(*hi_lo(d1)))
            w1[h] = w1f - u[:HEAD]
            b1[h] = b1v - u[HEAD + MB :]
            zq = z[2 * MB : 3 * MB] + z[3 * MB :] + b1v - u[HEAD : HEAD + MB]
            qact = gelu_parts(zq)[0]
            qahi, qalo = hi_lo(qact)
            left_e = rows2(qahi, qalo)
            uq = fold(mm_nt(left_e, rows2(ahi, ahi, ahi))) + mm_nt(qahi, rows2(alo, alo, alo))
            r3 = lanes3(e3 * (uq + 1.0))
            z2q = both_halves(fold(mm_nt(left_e, w2s))) + b2v - mm(r3, split3(d2hi, d2lo))
            invq = lax.rsqrt(mean_dup(z2q * z2q) + EPS)
            y = z2q * invq
            outs.append(q + gain * y + shift)
            ed2 = e * d2
            upd = mm(jnp.transpose(stack3(*hi_lo(ed2)))[:HEAD], split3(ahi, alo))
            w2[h] = w2f - upd
            b2[h] = b2v - jnp.sum(ed2, axis=0, keepdims=True)
            z1_ref[i, h] = z1
            zq_ref[i, h] = zq
            m_ref[i, h] = m
            d2_ref[i, h] = d2
            x_ref[i, h] = x
            y_ref[i, h] = y
            r_ref[i, h] = jnp.broadcast_to(inv, (MB, LANES))
            rq_ref[i, h] = jnp.broadcast_to(invq, (MB, LANES))
        out_ref[rows, :] = pack(outs)
        return carry

    lax.fori_loop(0, steps, step, 0)


def bwd_kernel(heads, steps, resets_ref, qkv_ref, rate_ref, cot_ref, gain_ref, shift_ref,
               s1_ref, s2_ref, z1_ref, zq_ref, m_ref, d2_ref, x_ref, y_ref, r_ref, rq_ref,
               dqkv_ref, de_ref, gw1, gb1, gw2, gb2, ggain, gshift,
               w1, b1, w2, b2):
    blocks = pl.num_programs(0)
    block = blocks - 1 - pl.program_id(0)

    @pl.when(pl.program_id(0) == 0)
    def _():
        for ref in (gw1, gb1, gw2, gb2, ggain, gshift, w1, b1, w2, b2):
            ref[...] = jnp.zeros_like(ref)

    def step(back, carry):
        i = steps - 1 - back
        at = block * steps + i
        rows = pl.ds(pl.multiple_of(i * MB, MB), MB)
        qkv = qkv_ref[rows, :]
        rates = rate_ref[rows, :]
        cots = cot_ref[rows, :]
        lane = lane_of((MB, LANES))
        lane48 = lane_of((MB, 3 * MB))
        row48 = lax.broadcasted_iota(jnp.int32, (MB, 3 * MB), 0)
        causal3 = row48 <= lax.rem(lane48, MB)
        dqs, dks, dvs = [], [], []
        de_all = jnp.zeros((MB, LANES), F32)
        for h in range(heads):
            gain = gain_ref[h]
            shift = shift_ref[h]
            gain2 = gain * gain
            q = pick(qkv, h)
            k = pick(qkv, heads + h)
            v = pick(qkv, 2 * heads + h)
            cot = pick(cots, h)
            ecol = rates[:, h : h + 1]
            e = jnp.broadcast_to(ecol, (MB, LANES))
            e256 = jnp.broadcast_to(ecol, (MB, INNER))
            e3 = jnp.where(causal3, jnp.broadcast_to(ecol, (MB, 3 * MB)), 0.0)
            khi, klo = hi_lo(k)
            qhi, qlo = hi_lo(q)
            left_k = rows2(khi, klo)
            qsplit = jnp.where(lane < HEAD, qhi.astype(F32), qlo.astype(F32)).astype(BF16)
            kq3 = fold(mm_nt(left_k, rows2(qsplit, qsplit, qsplit))) + 1.0
            pt3 = lanes3(e3 * kq3)
            ones = jnp.where(lane < HEAD + MB, 1.0, 0.0)
            qone = hi_lo(jnp.where(lane < HEAD, q, ones))
            kone = hi_lo(jnp.where(lane < HEAD, k, ones))
            left_q = jnp.transpose(rows2(stack3(*qone), stack3(*kone)))[: HEAD + MB]

            s1 = s1_ref[i, h]
            s2 = s2_ref[i, h]
            z1 = z1_ref[i, h]
            zq = zq_ref[i, h]
            m = m_ref[i, h]
            d2 = d2_ref[i, h]
            x = x_ref[i, h]
            y = y_ref[i, h]
            inv = r_ref[i, h]
            invq = rq_ref[i, h]
            act, slope, t, zs, sech, inner = gelu_parts(z1)
            curve = gelu_curve(z1, t, zs, sech, inner)
            qact, qslope = gelu_parts(zq)[:2]
            ahi, alo = hi_lo(act)
            qahi, qalo = hi_lo(qact)
            d1 = m * slope

            dy = gain * cot
            dz2q = invq * (dy - mean_dup(dy) - y * mean_dup(dy * y))
            ggain_part = cot * y
            zhi, zlo = hi_lo(dz2q)
            dqa = fold(mm(rows2(zhi, zlo), s2))
            left_a = rows2(ahi, alo)
            aq3 = fold(mm_nt(left_a, rows2(qahi, qahi, qahi))) + mm_nt(ahi, rows2(qalo, qalo, qalo)) + 1.0
            rt3 = lanes3(e3 * aq3)
            d2hi, d2lo = hi_lo(d2)
            zsplit = jnp.where(lane < HEAD, zhi.astype(F32), zlo.astype(F32)).astype(BF16)
            drt3 = -fold(mm_nt(rows2(d2hi, d2lo), rows2(zsplit, zsplit, zsplit)))
            third = lane48 < MB
            de = jnp.sum(jnp.where(causal3 & third, drt3 * aq3, 0.0), axis=1, keepdims=True)
            du2t = e3 * drt3
            du2t_hi, du2t_lo = hi_lo(du2t[:, :MB])
            dqa = dqa + mm_tn(rows2(du2t_hi, du2t_lo, du2t_hi), split3(ahi, alo))
            da = mm(lanes3(du2t), split3(qahi, qalo))
            dzq = dqa * qslope
            zqhi, zqlo = hi_lo(dzq)
            d1hi, d1lo = hi_lo(d1)
            dpt3 = -(fold(mm_nt(rows2(d1hi, d1lo), rows2(zqhi, zqhi, zqhi))) + mm_nt(d1hi, rows2(zqlo, zqlo, zqlo)))
            de = de + jnp.sum(jnp.where(causal3 & third, dpt3 * kq3, 0.0), axis=1, keepdims=True)
            du1t = e3 * dpt3
            du1t_hi, du1t_lo = hi_lo(du1t[:, :MB])
            dq = cot + mm_tn(rows2(du1t_hi, du1t_lo, du1t_hi), split3(khi, klo))
            dk = mm(lanes3(du1t), split3(qhi, qlo))
            zq3 = split3(zqhi, zqlo)
            dd1 = -mm(pt3, zq3)
            dd2 = -mm(rt3, split3(zhi, zlo))

            w1f = w1[h]
            w2f = w2[h]
            b1v = b1[h]
            b2v = b2[h]
            w1s = rows2(*hi_lo(w1f))
            w2s = rows2(*hi_lo(w2f))
            de1 = -(fold(mm(left_k, w1s)) + b1v)
            de = de + jnp.sum(d1 * de1, axis=1, keepdims=True)
            dd1 = dd1 + e256 * de1
            ed1 = e256 * d1
            dkw = -fold(mm_nt(rows2(*hi_lo(ed1)), w1s))
            de2 = -(both_halves(fold(mm_nt(left_a, w2s))) + b2v)
            de = de + 0.5 * jnp.sum(d2 * de2, axis=1, keepdims=True)
            ed2 = e * d2
            da = da - fold(mm(rows2(*hi_lo(ed2)), w2s))
            dm = dd1 * slope
            dz1 = dd1 * m * curve
            dmhi, dmlo = hi_lo(dm)
            dd2 = dd2 + e * de2 + both_halves(fold(mm_nt(rows2(dmhi, dmlo), s2)))

            coef = gain * (shift - v + k)
            g = gain2 * x + coef
            mg = mean_dup(g)
            mgx = mean_dup(g * x)
            q1 = mean_dup(dd2)
            q2 = mean_dup(dd2 * x)
            dr_r = 2.0 * HEAD * 0.5 * mean_dup(dd2 * d2)
            dg = inv * (dd2 - q1 - x * q2)
            dx = dg * gain2 - inv * (dd2 * mgx + g * q2)
            ggain_part = ggain_part + dg * (2.0 * gain * x + shift - v + k)
            dgg = dg * gain
            dz2 = inv * (dx - mean_dup(dx) - x * mean_dup(dx * x)) - x * inv * (dr_r * (1.0 / HEAD))
            dz2hi, dz2lo = hi_lo(dz2)
            da = da + fold(mm(rows2(dz2hi, dz2lo), s2))
            dz1 = dz1 + da * slope
            z1hi, z1lo = hi_lo(dz1)
            grads = mm(left_q, rows2(zq3, split3(z1hi, z1lo)))
            to_rows = mm_nt(rows2(zqhi, zqlo, z1hi, z1lo), s1)
            dq = dq + both_halves(fold(to_rows[: 2 * MB]))
            dk = dk + dgg + both_halves(dkw + fold(to_rows[2 * MB :]))
            left_2 = jnp.transpose(rows2(stack3(zhi, zlo), stack3(d2hi, d2lo), stack3(dz2hi, dz2lo)))[:HEAD]
            grads2 = mm(left_2, rows2(split3(qahi, qalo), split3(dmhi, dmlo), split3(ahi, alo)))
            w1[h] = w1f + grads[:HEAD]
            b1[h] = b1v + grads[HEAD:]
            w2[h] = w2f + grads2
            b2[h] = b2v + jnp.sum(dz2q + dz2, axis=0, keepdims=True)
            ggain[h] += ggain_part
            gshift[h] += cot + dgg
            dqs.append(dq)
            dks.append(dk)
            dvs.append(-dgg)
            de_all = jnp.where(lane == h, de, de_all)
        dqkv_ref[rows, :] = pack(dqs + dks + dvs)
        de_ref[rows, :] = de_all

        @pl.when(resets_ref[at] == 1)
        def _():
            gw1[...] += w1[...]
            gb1[...] += b1[...]
            gw2[...] += w2[...]
            gb2[...] += b2[...]
            for ref in (w1, b1, w2, b2):
                ref[...] = jnp.zeros_like(ref)

        return carry

    lax.fori_loop(0, steps, step, 0)


def tiles_of(count):
    return -(-count // 2) * LANES


def state_scratch(heads):
    return [
        pltpu.VMEM((heads, HEAD, INNER), F32),
        pltpu.VMEM((heads, MB, INNER), F32),
        pltpu.VMEM((heads, HEAD, INNER), F32),
        pltpu.VMEM((heads, MB, LANES), F32),
    ]


def saved_shapes(total, heads):
    return [
        ((total, heads, LANES, INNER), BF16),
        ((total, heads, LANES, INNER), BF16),
        ((total, heads, MB, INNER), F32),
        ((total, heads, MB, INNER), F32),
        ((total, heads, MB, INNER), F32),
        ((total, heads, MB, LANES), F32),
        ((total, heads, MB, LANES), F32),
        ((total, heads, MB, LANES), F32),
        ((total, heads, MB, LANES), F32),
        ((total, heads, MB, LANES), F32),
    ]


def whole_spec(shape):
    zeros = (0,) * len(shape)
    return pl.BlockSpec(shape, lambda i, *_: zeros)


def chain_forward(resets, qkv, rates, gain, shift, w1i, b1i, w2i, b2i, steps=8, interpret=False):
    heads = gain.shape[0]
    total = resets.shape[0]
    blocks = total // steps
    token_spec = lambda width: pl.BlockSpec((steps * MB, width), lambda i, *_: (i, 0))
    saved = saved_shapes(total, heads)
    saved_specs = [pl.BlockSpec((steps,) + s[1:], lambda i, *_: (i, 0, 0, 0)) for s, _ in saved]
    params = (gain, shift, w1i, b1i, w2i, b2i)
    out = pl.pallas_call(
        functools.partial(fwd_kernel, heads, steps),
        grid_spec=pltpu.PrefetchScalarGridSpec(
            num_scalar_prefetch=1,
            grid=(blocks,),
            in_specs=[token_spec(qkv.shape[1]), token_spec(LANES)] + [whole_spec(p.shape) for p in params],
            out_specs=[token_spec(tiles_of(heads))] + saved_specs,
            scratch_shapes=state_scratch(heads),
        ),
        out_shape=[jax.ShapeDtypeStruct((total * MB, tiles_of(heads)), F32)] + [jax.ShapeDtypeStruct(s, d) for s, d in saved],
        compiler_params=pltpu.CompilerParams(dimension_semantics=("arbitrary",), vmem_limit_bytes=56 * 1024 * 1024),
        interpret=interpret,
    )(resets, qkv, rates, *params)
    return out[0], out[1:]


def chain_backward(resets, qkv, rates, cot, gain, shift, saved, steps=8, interpret=False):
    heads = gain.shape[0]
    total = resets.shape[0]
    blocks = total // steps
    token_spec = lambda width: pl.BlockSpec((steps * MB, width), lambda i, *_: (blocks - 1 - i, 0))
    saved_specs = [pl.BlockSpec((steps,) + s.shape[1:], lambda i, *_: (blocks - 1 - i, 0, 0, 0)) for s in saved]
    acc_shapes = [(heads, HEAD, INNER), (heads, MB, INNER), (heads, HEAD, INNER), (heads, MB, LANES), (heads, MB, LANES), (heads, MB, LANES)]
    return pl.pallas_call(
        functools.partial(bwd_kernel, heads, steps),
        grid_spec=pltpu.PrefetchScalarGridSpec(
            num_scalar_prefetch=1,
            grid=(blocks,),
            in_specs=[token_spec(qkv.shape[1]), token_spec(LANES), token_spec(cot.shape[1]), whole_spec(gain.shape), whole_spec(shift.shape)] + saved_specs,
            out_specs=[token_spec(qkv.shape[1]), token_spec(LANES)] + [whole_spec(s) for s in acc_shapes],
            scratch_shapes=state_scratch(heads),
        ),
        out_shape=[jax.ShapeDtypeStruct(qkv.shape, F32), jax.ShapeDtypeStruct((total * MB, LANES), F32)]
        + [jax.ShapeDtypeStruct(s, F32) for s in acc_shapes],
        compiler_params=pltpu.CompilerParams(dimension_semantics=("arbitrary",), vmem_limit_bytes=56 * 1024 * 1024),
        interpret=interpret,
    )(resets, qkv, rates, cot, gain, shift, *saved)


HEADS = 12
base_rate = 0.1
high = lax.Precision.HIGH


def dot(left, right):
    return jnp.dot(left, right, precision=high)


def dot_t(left, right):
    return lax.dot_general(left, right, (((1,), (1,)), ((), ())), precision=high)


def t_dot(left, right):
    return lax.dot_general(left, right, (((0,), (0,)), ((), ())), precision=high)


def swap(value, axis, mask):
    count = lax.axis_size(axis)
    return lax.ppermute(value, axis, [(source, source ^ mask) for source in range(count)])


def bits_of(axis):
    count = lax.axis_size(axis)
    return [1 << at for at in reversed(range(count.bit_length() - 1))]


def gather(value, axis):
    me = lax.axis_index(axis)
    shape = value.shape
    for done, mask in enumerate(bits_of(axis)):
        other = swap(value, axis, mask)
        upper = (me & mask) != 0
        value = jnp.stack([jnp.where(upper, other, value), jnp.where(upper, value, other)], axis=done)
    return value.reshape((-1,) + shape)


def scatter_sum(value, axis):
    me = lax.axis_index(axis)
    masks = bits_of(axis)
    value = value.reshape((2,) * len(masks) + value.shape[1:])
    for mask in reversed(masks):
        last = masks.index(mask)
        upper = (me & mask) != 0
        lower_half = lax.index_in_dim(value, 0, last, keepdims=False)
        upper_half = lax.index_in_dim(value, 1, last, keepdims=False)
        other = swap(jnp.where(upper, lower_half, upper_half), axis, mask)
        value = jnp.where(upper, upper_half, lower_half) + other
    return value


def sum_over(value, axis):
    for mask in reversed(bits_of(axis)):
        value = value + swap(value, axis, mask)
    return value


def columns_to_tokens(value, groups, width):
    n = lax.axis_size("seq")
    tokens = value.shape[0] // n
    moved = lax.all_to_all(value.reshape(n, tokens, -1), "seq", 0, 0)
    moved = moved.reshape(n, tokens, groups, -1).transpose(1, 2, 0, 3)
    return moved.reshape(tokens, groups, -1)[:, :, :width]


def tokens_to_columns(value):
    n = lax.axis_size("seq")
    tokens = value.shape[0]
    moved = lax.all_to_all(value.reshape(tokens, n, -1).transpose(1, 0, 2), "seq", 0, 0)
    return moved.reshape(n * tokens, -1)


def doc_masks(lengths, span):
    block_counts = (lengths + MB - 1) // MB
    begins = jnp.cumsum(block_counts, dtype=jnp.int32) - block_counts
    block_index = jnp.arange(span // MB, dtype=jnp.int32)
    resets = jnp.any(block_index[:, None] == begins[None, :], axis=1).astype(jnp.int32)
    positions = jnp.arange(span, dtype=jnp.int32)
    starts = begins * MB
    inside = (positions[:, None] >= starts[None, :]) & (positions[:, None] < (starts + lengths)[None, :])
    return resets, jnp.any(inside, axis=1).astype(F32)


def own_heads(value, axis, per_head, groups=1):
    n = lax.axis_size("seq")
    me = lax.axis_index("seq")
    count = -(-HEADS // n)
    shape = value.shape
    value = value.reshape(shape[:axis] + (groups, HEADS * per_head) + shape[axis + 1 :])
    pads = [(0, 0)] * value.ndim
    pads[axis + 1] = (0, (n * count - HEADS) * per_head)
    value = jnp.pad(value, pads)
    value = lax.dynamic_slice_in_dim(value, me * count * per_head, count * per_head, axis + 1)
    return value.reshape(shape[:axis] + (groups * count * per_head,) + shape[axis + 1 :])


def pad_columns(value, width):
    return jnp.pad(value, ((0, 0), (0, width - value.shape[1])))


def local(
    layer_input,
    doc_lengths,
    output_grad,
    mixer_gain,
    triple_weight,
    rate_weight,
    rate_bias,
    first_weight,
    first_bias,
    second_weight,
    second_bias,
    inner_gain,
    inner_shift,
    gate_weight,
    output_weight,
    feed_gain,
    feed_weight,
    down_weight,
):
    n = lax.axis_size("seq")
    n_rows = lax.axis_size("rows")
    me = lax.axis_index("seq")
    heads = -(-HEADS // n)
    _, tokens, width = layer_input.shape
    span = tokens * n
    ff = down_weight.shape[0]
    x = layer_input[0]
    cot = output_grad[0]
    resets, valid = doc_masks(doc_lengths[0], span)

    inv = lax.rsqrt(jnp.mean(x * x, axis=-1, keepdims=True) + EPS)
    xhat = x * inv
    normed = xhat * mixer_gain
    normed_row = gather(normed, "seq").reshape(span, width)
    own_triple = own_heads(triple_weight, 1, HEAD, 3)
    own_gate = own_heads(gate_weight, 1, HEAD)
    own_rate = own_heads(rate_weight, 1, 1)
    qkv = dot(normed_row, pad_columns(own_triple, tiles_of(3 * heads)))
    rate_sig = jax.nn.sigmoid(dot(normed_row, pad_columns(own_rate, LANES)) + jnp.pad(own_heads(rate_bias, 0, 1), (0, LANES - heads)))
    rates = (base_rate / HEAD) * rate_sig * valid[:, None]

    def per_head(value, rows, axis):
        value = own_heads(value, 0, 1)
        return jnp.broadcast_to(jnp.concatenate([value] * axis, axis=1)[:, None, :], (heads, rows, value.shape[1] * axis))

    gain = per_head(inner_gain, MB, 2)
    shift = per_head(inner_shift, MB, 2)
    w1i = own_heads(first_weight, 0, 1)
    b1i = per_head(first_bias, MB, 1)
    w2t = own_heads(second_weight, 0, 1).transpose(0, 2, 1)
    w2i = w2t - jnp.mean(w2t, axis=1, keepdims=True)
    b2i = per_head(second_bias - jnp.mean(second_bias, axis=1, keepdims=True), MB, 2)
    mixed, saved = chain_forward(resets, qkv, rates, gain, shift, w1i, b1i, w2i, b2i)
    mixed = mixed[:, : heads * HEAD]

    gate_pre = dot(normed_row, own_gate)
    gate_act, gate_slope = gelu_parts(gate_pre)[:2]
    gated = columns_to_tokens(gate_act * mixed, 1, width)[:, 0]
    middle = x + dot(gated, output_weight)
    inv2 = lax.rsqrt(jnp.mean(middle * middle, axis=-1, keepdims=True) + EPS)
    mhat = middle * inv2
    second = mhat * feed_gain
    both = dot(second, feed_weight)
    left, right = both[:, :ff], both[:, ff:]
    sig = jax.nn.sigmoid(left)
    silu = left * sig
    hidden = silu * right
    layer_output = middle + dot(hidden, down_weight)

    dhidden = dot_t(cot, down_weight)
    dboth = jnp.concatenate([dhidden * right * (sig + silu * (1.0 - sig)), dhidden * silu], axis=1)
    dsecond = dot_t(dboth, feed_weight)
    feed_gain_part = jnp.sum(dsecond * mhat, axis=0)
    dmhat = dsecond * feed_gain
    dmiddle = cot + inv2 * (dmhat - mhat * jnp.mean(dmhat * mhat, axis=-1, keepdims=True))
    dgated = tokens_to_columns(pad_columns(dot_t(dmiddle, output_weight), n * heads * HEAD))
    dmixed = pad_columns(dgated * gate_act, tiles_of(heads))
    dgate = dgated * mixed * gate_slope

    second_row = gather(second, "seq").reshape(span, width)
    dboth_cols = tokens_to_columns(dboth)
    feed_part = t_dot(second_row, dboth_cols)
    down_part = scatter_sum(jnp.stack(jnp.split(t_dot(hidden, cot), n, axis=1)), "seq")
    output_part = scatter_sum(jnp.stack(jnp.split(t_dot(gated, dmiddle), n, axis=1)), "seq")

    def over_rows(part):
        return scatter_sum(part.reshape((n_rows, part.shape[0] // n_rows) + part.shape[1:]), "rows")

    feed_weight_grad = over_rows(feed_part)
    down_weight_grad = over_rows(down_part)
    output_weight_grad = over_rows(output_part)

    dqkv, drate, gw1, gb1, gw2, gb2, ggain, gshift = chain_backward(resets, qkv, rates, dmixed, gain, shift, saved)
    dqkv = dqkv[:, : 3 * heads * HEAD]
    dpre = drate[:, :heads] * rates[:, :heads] * (1.0 - rate_sig[:, :heads])

    dcols = jnp.concatenate([dqkv, dgate], axis=1)
    weights_part = t_dot(normed_row, dcols)
    rate_part = t_dot(normed_row, dpre)
    weights_sum = over_rows(weights_part)
    all_cols = gather(weights_sum, "seq").reshape(n, weights_sum.shape[0], 4, heads * HEAD)
    all_cols = all_cols.transpose(1, 2, 0, 3).reshape(weights_sum.shape[0], 4, -1)[:, :, :width]
    triple_all = all_cols[:, :3].reshape(weights_sum.shape[0], 3 * width)
    triple_weight_grad = lax.dynamic_slice_in_dim(triple_all, me * (3 * width // n), 3 * width // n, 1)
    gate_weight_grad = lax.dynamic_slice_in_dim(all_cols[:, 3], me * (width // n), width // n, 1)

    dtokens = columns_to_tokens(dcols, 4, width)
    drates = columns_to_tokens(dpre, 1, HEADS)[:, 0]
    dnormed = dot_t(dtokens[:, :3].reshape(tokens, 3 * width), triple_weight) + dot_t(dtokens[:, 3], gate_weight)
    dnormed = dnormed + dot_t(drates, rate_weight)
    mixer_gain_part = jnp.sum(dnormed * xhat, axis=0)
    dxhat = dnormed * mixer_gain
    input_grad = dmiddle + inv * (dxhat - xhat * jnp.mean(dxhat * xhat, axis=-1, keepdims=True))

    head_parts = [
        rate_part.T,
        jnp.sum(dpre, axis=0)[:, None],
        gw1,
        gb1[:, 0],
        gw2.transpose(0, 2, 1),
        gb2[:, 0, :HEAD],
        jnp.sum(ggain, axis=1)[:, :HEAD],
        jnp.sum(gshift, axis=1)[:, :HEAD],
    ]
    shapes = [part.shape for part in head_parts]
    flat = jnp.concatenate([part.reshape(heads, -1) for part in head_parts], axis=1)
    size = flat.size
    flat = jnp.pad(flat.reshape(-1), (0, -size % (n_rows * LANES * 8))).reshape(n_rows, -1, LANES)
    flat = gather(scatter_sum(flat, "rows"), "rows").reshape(-1)[:size].reshape(heads, -1)
    flat = gather(flat, "seq").reshape(n * heads, -1)[:HEADS]
    head_grads = []
    start = 0
    for shape in shapes:
        count = 1
        for extent in shape[1:]:
            count *= extent
        head_grads.append(flat[:, start : start + count].reshape((HEADS,) + shape[1:]))
        start += count
    gains = sum_over(sum_over(jnp.stack([mixer_gain_part, feed_gain_part]), "seq"), "rows")

    return (
        layer_output[None],
        input_grad[None],
        gains[0],
        triple_weight_grad,
        head_grads[0].T,
        head_grads[1][:, 0],
        head_grads[2],
        head_grads[3],
        head_grads[4],
        head_grads[5],
        head_grads[6],
        head_grads[7],
        gate_weight_grad,
        output_weight_grad,
        gains[1],
        feed_weight_grad,
        down_weight_grad,
    )


def solution(mesh):
    tokens = P("rows", "seq", None)
    shard = P("rows", "seq")
    in_specs = (tokens, P("rows", None), tokens) + (P(),) * 15
    out_specs = (tokens, tokens, P(), shard) + (P(),) * 8 + (shard, shard, P(), shard, shard)
    return jax.shard_map(local, mesh=mesh, in_specs=in_specs, out_specs=out_specs, check_vma=False)
```

```python
import functools
import jax
import jax.numpy as jnp
from jax import lax
from jax.experimental import pallas as pl
from jax.experimental.pallas import tpu as pltpu
from jax.sharding import PartitionSpec as P

HEAD = 64
INNER = 256
MB = 16
EPS = 1e-06
RTP = 0.7978845608028654
F32 = jnp.float32
BF16 = jnp.bfloat16
LANES = 128
BASE_RATE = 0.1
FWD_COST = 1_500_000_000
BWD_COST = 2_000_000_000


def hi_lo(value):
    high = value.astype(BF16)
    return high, (value - high.astype(F32)).astype(BF16)


def hi_mid_lo(value):
    high = value.astype(BF16)
    rest = value - high.astype(F32)
    mid = rest.astype(BF16)
    return high, mid, (rest - mid.astype(F32)).astype(BF16)


def fold_all(value):
    total = value[:MB]
    for at in range(MB, value.shape[0], MB):
        total = total + value[at : at + MB]
    return total


def six_left(high, mid, low):
    return rows2(high, high, high, mid, mid, low)


def six_right(high, mid, low):
    return rows2(high, mid, low, high, mid, high)


def three_times(value):
    return jnp.concatenate([value, value[:, :HEAD]], axis=1)


def mm(left, right):
    return lax.dot_general(left, right, (((1,), (0,)), ((), ())), preferred_element_type=F32)


def mm_nt(left, right):
    return lax.dot_general(left, right, (((1,), (1,)), ((), ())), preferred_element_type=F32)


def mm_tn(left, right):
    return lax.dot_general(left, right, (((0,), (0,)), ((), ())), preferred_element_type=F32)


def rows2(*parts):
    return jnp.concatenate(parts, axis=0)


def fold(value):
    return value[:MB] + value[MB:]


def half_turn(value):
    return pltpu.roll(value, HEAD, 1)


def both_halves(value):
    return value + half_turn(value)


def lane_of(shape):
    return lax.broadcasted_iota(jnp.int32, shape, 1)


def pick(block, unit):
    tile = block[:, (unit // 2) * LANES : (unit // 2 + 1) * LANES]
    turned = half_turn(tile)
    low_half = lane_of(tile.shape) < HEAD
    if unit % 2 == 0:
        return jnp.where(low_half, tile, turned)
    return jnp.where(low_half, turned, tile)


def pack(parts):
    tiles = []
    for at in range(0, len(parts), 2):
        left = parts[at]
        right = parts[at + 1] if at + 1 < len(parts) else jnp.zeros_like(left)
        tiles.append(jnp.where(lane_of(left.shape) < HEAD, left, right))
    return jnp.concatenate(tiles, axis=1) if len(tiles) > 1 else tiles[0]


def mean_dup(value):
    return jnp.sum(value, axis=1, keepdims=True) * (1.0 / LANES)


def gelu_parts(z):
    z2 = z * z
    t = jnp.tanh(z * (RTP + (RTP * 0.044715) * z2))
    one_t = 0.5 + 0.5 * t
    sech = (1.0 - t) * one_t
    inner = RTP + (RTP * 0.134145) * z2
    act = z * one_t
    zs = z * sech
    slope = one_t + zs * inner
    return act, slope, t, zs, sech, inner


def gelu_curve(z, t, zs, sech, inner):
    return 2.0 * sech * inner + zs * ((2.0 * RTP * 0.134145) * z) - 2.0 * t * zs * inner * inner


def split3(high, low):
    return rows2(high, high, low)


def stack3(high, low):
    return rows2(high, low, high)


def lanes3(value):
    high, low = hi_lo(value)
    lane = lane_of(value.shape)
    return jnp.where((lane >= MB) & (lane < 2 * MB), low.astype(F32), high.astype(F32)).astype(BF16)


def interleave(works):
    works = list(works)
    while works:
        for work in list(works):
            try:
                next(work)
            except StopIteration:
                works.remove(work)


def rates_of(cols, bias_ref, heads, count):
    unit = 3 * heads
    tile = cols[:, (unit // 2) * LANES : (unit // 2 + 1) * LANES] + bias_ref[:1]
    sig = 0.5 + 0.5 * jnp.tanh(0.5 * tile)
    row = lax.broadcasted_iota(jnp.int32, tile.shape, 0)
    return jnp.where(row < count, (BASE_RATE / HEAD) * sig, 0.0), sig, HEAD * (unit % 2)


def put(refs, head, *values):
    for ref, value in zip(refs, values, strict=True):
        ref[head] = value


def take(refs, head):
    return [ref[head] for ref in refs]


def spread_lanes(column, width=LANES):
    return jnp.broadcast_to(column, (MB, width))


def fwd_ready(heads):
    shapes = [((5 * MB, 3 * HEAD), BF16), ((HEAD + 2 * MB, 3 * MB), BF16), ((MB, 3 * MB), F32)] + [((MB, LANES), F32)] * 4
    return [pltpu.VMEM((heads,) + shape, dtype) for shape, dtype in shapes]


def fwd_left(heads):
    shapes = [((2 * MB, INNER), BF16), ((2 * MB, LANES), BF16), ((MB, 3 * MB), F32), ((MB, LANES), F32), ((MB, LANES), F32)]
    return [pltpu.VMEM((heads,) + shape, dtype) for shape, dtype in shapes]


def fwd_kernel(heads, steps, resets_ref, counts_ref, qkv_ref, gate_ref, bias_ref, gain_ref, shift_ref, w1i, b1i, w2i, b2i,
               gated_ref, mixed_ref, s1_ref, s2_ref, z1_ref, zq_ref, m_ref, d2_ref, x_ref, y_ref, r_ref, rq_ref,
               w1, b1, w2, b2, *ready):
    block = pl.program_id(0)
    count = len(fwd_ready(heads))
    ready, left = (ready[:count], ready[count : 2 * count]), ready[2 * count :]
    left = (left[: len(left) // 2], left[len(left) // 2 :])
    lane = lane_of((MB, LANES))
    row = lax.broadcasted_iota(jnp.int32, (MB, LANES), 0)
    lane48 = lane_of((MB, 3 * MB))
    row48 = lax.broadcasted_iota(jnp.int32, (MB, 3 * MB), 0)
    causal = (lane >= HEAD) & (lane < HEAD + MB) & (row <= lane - HEAD)

    def rows_of(i):
        return pl.ds(pl.multiple_of(i * MB, MB), MB)

    def prepare(i, refs):
        qkv = qkv_ref[rows_of(i), :]
        rates, _, rate_lane = rates_of(qkv, bias_ref, heads, counts_ref[block * steps + i])

        def work(h):
            q = pick(qkv, h)
            k = pick(qkv, heads + h)
            v = pick(qkv, 2 * heads + h)
            e = spread_lanes(rates[:, rate_lane + h : rate_lane + h + 1])
            yield
            coef = gain_ref[h] * (shift_ref[h] - v + k)
            khi, klo = hi_lo(k)
            qhi, qlo = hi_lo(q)
            left_a = three_times(rows2(*hi_mid_lo(k), qhi, qlo))
            qsplit = jnp.where(lane < HEAD, qhi.astype(F32), qlo.astype(F32)).astype(BF16)
            zero = jnp.zeros((HEAD, LANES), BF16)
            kq = fold(mm_nt(rows2(khi, klo), rows2(zero, qsplit, zero[: HEAD - MB])))
            yield
            left_d = e * jnp.where(lane < HEAD, k, jnp.where(causal, kq + 1.0, jnp.where((lane >= HEAD + MB) & (lane < HEAD + 2 * MB), 1.0, 0.0)))
            left_d3 = jnp.transpose(stack3(*hi_lo(left_d)))[: HEAD + 2 * MB]
            erow = jnp.transpose(e)[:MB, :]
            e3 = jnp.where(lax.rem(lane48, MB) <= row48, jnp.concatenate([erow, erow, erow], axis=1), 0.0)
            yield
            put(refs, h, left_a, left_d3, e3, e, q, coef, spread_lanes(mean_dup(coef)))

        return [work(h) for h in range(heads)]

    def advance(i, refs, left):
        def work(h):
            left_a, left_d3, e3, e, q, coef, coef_mean = take(refs, h)
            gain = gain_ref[h]
            gain2 = gain * gain
            w1f = w1[h]
            w2f = w2[h]
            w1s = rows2(*hi_mid_lo(w1f))
            w2hi, w2mid, w2lo = hi_mid_lo(w2f)
            w2s = rows2(w2hi, w2mid)
            s1_ref[i, h] = w1s[: 2 * HEAD]
            s2_ref[i, h] = w2s
            b1v = b1[h]
            b2v = b2[h]
            z = mm(left_a, w1s)
            yield
            z1 = fold_all(z[: 3 * MB]) + b1v
            act, slope = gelu_parts(z1)[:2]
            ahi, alo, arest = hi_mid_lo(act)
            z2 = fold_all(mm_nt(rows2(ahi, alo, arest), rows2(w2s, w2lo, jnp.zeros((HEAD, INNER), BF16))))
            yield
            z2 = both_halves(z2[:, :LANES] + z2[:, LANES:]) + b2v
            yield
            g2z = gain2 * z2
            inv = lax.rsqrt(mean_dup(z2 * z2) + EPS)
            m1 = mean_dup(g2z)
            m2 = mean_dup(g2z * z2)
            m3 = mean_dup(coef * z2)
            yield
            x = z2 * inv
            g = gain2 * x + coef
            d2 = inv * (g - (inv * m1 + coef_mean) - x * (inv * inv * m2 + inv * m3))
            d2hi, d2lo = hi_lo(d2)
            m = fold(mm(rows2(d2hi, d2lo), w2s))
            yield
            d1 = m * slope
            u = mm(left_d3, split3(*hi_lo(d1)))
            yield
            w1[h] = w1f - u[:HEAD]
            b1[h] = b1v - u[HEAD + MB :]
            ed2 = e * d2
            w2[h] = w2f - mm(jnp.transpose(six_left(*hi_mid_lo(ed2)))[:HEAD], six_right(ahi, alo, arest))
            b2[h] = b2v - jnp.sum(ed2, axis=0, keepdims=True)
            z1_ref[i, h] = z1
            zq_ref[i, h] = fold(z[3 * MB :]) + b1v - u[HEAD : HEAD + MB]
            m_ref[i, h] = m
            d2_ref[i, h] = d2
            x_ref[i, h] = x
            r_ref[i, h] = spread_lanes(inv)
            put(left, h, rows2(ahi, alo), rows2(d2hi, d2lo), e3, q, b2v)

        return [work(h) for h in range(heads)]

    def finish(i, left, outs):
        def work(h):
            left_b, left_c, e3, q, b2v = take(left, h)
            ahi, alo = left_b[:MB], left_b[MB:]
            w2s = s2_ref[i, h]
            qact = gelu_parts(zq_ref[i, h])[0]
            qahi, qalo = hi_lo(qact)
            left_e = rows2(qahi, qalo)
            uq = fold(mm_nt(left_e, rows2(ahi, ahi, ahi))) + mm_nt(qahi, rows2(alo, alo, alo))
            z2q = fold(mm_nt(left_e, w2s))
            yield
            r3 = lanes3(e3 * (uq + 1.0))
            z2q = both_halves(z2q) + b2v - mm(r3, split3(left_c[:MB], left_c[MB:]))
            yield
            invq = lax.rsqrt(mean_dup(z2q * z2q) + EPS)
            yield
            y = z2q * invq
            outs[h] = q + gain_ref[h] * y + shift_ref[h]
            y_ref[i, h] = y
            rq_ref[i, h] = spread_lanes(invq)

        return [work(h) for h in range(heads)]

    def store(i, outs):
        mixed = pack(outs)
        mixed_ref[rows_of(i), :] = mixed
        gated_ref[rows_of(i), :] = gelu_parts(gate_ref[rows_of(i), :])[0] * mixed

    def step(i, now, later, parity):
        @pl.when(resets_ref[block * steps + i] == 1)
        def _():
            w1[...] = w1i[...]
            b1[...] = b1i[...]
            w2[...] = w2i[...]
            b2[...] = b2i[...]

        outs = [None] * heads
        behind = jnp.maximum(i - 1, 0)
        interleave(advance(i, now, left[parity]) + finish(behind, left[1 - parity], outs) + prepare(jnp.minimum(i + 1, steps - 1), later))
        store(behind, outs)

    interleave(prepare(0, ready[0]))

    def pair(at, carry):
        step(2 * at, ready[0], ready[1], 0)
        step(2 * at + 1, ready[1], ready[0], 1)
        return carry

    lax.fori_loop(0, steps // 2, pair, 0)
    outs = [None] * heads
    interleave(finish(steps - 1, left[1], outs))
    store(steps - 1, outs)


def bwd_ready(heads):
    halves = [(2 * MB, LANES), (HEAD + MB, 6 * MB), (2 * MB, INNER), (2 * MB, INNER), (2 * MB, INNER), (2 * MB, INNER), (2 * MB, LANES), (HEAD, 6 * MB)]
    wide = [(MB, INNER)] * 4
    rest = [(MB, LANES)] * 11
    shapes = [(shape, BF16) for shape in halves] + [(shape, F32) for shape in wide + rest]
    return [pltpu.VMEM((heads,) + shape, dtype) for shape, dtype in shapes]


def bwd_kernel(heads, steps, first_block, begun, resets_ref, counts_ref, qkv_ref, bias_ref, cot_ref, gain_ref, shift_ref,
               s1_ref, s2_ref, z1_ref, zq_ref, m_ref, d2_ref, x_ref, y_ref, r_ref, rq_ref, *refs):
    before = refs[:10] if begun else None
    dqkv_ref, w1, b1, w2, b2, gw1, gb1, gw2, gb2, ggain, gshift, *ready = refs[10 if begun else 0 :]
    count = len(ready) // 2
    ready = (ready[:count], ready[count:])
    blocks = pl.num_programs(0)
    block = first_block + blocks - 1 - pl.program_id(0)
    lane = lane_of((MB, LANES))
    lane48 = lane_of((MB, 3 * MB))
    row48 = lax.broadcasted_iota(jnp.int32, (MB, 3 * MB), 0)
    causal3 = row48 <= lax.rem(lane48, MB)
    counted = causal3 & (lane48 < MB)

    @pl.when(pl.program_id(0) == 0)
    def _():
        for at, ref in enumerate((w1, b1, w2, b2, gw1, gb1, gw2, gb2, ggain, gshift)):
            ref[...] = before[at][...] if begun else jnp.zeros_like(ref)

    def rows_of(i):
        return pl.ds(pl.multiple_of(i * MB, MB), MB)

    def rates_at(i, qkv):
        return rates_of(qkv, bias_ref, heads, counts_ref[block * steps + i])

    def prepare(i, refs):
        qkv = qkv_ref[rows_of(i), :]
        rates, sigs, rate_lane = rates_at(i, qkv)
        cots = cot_ref[rows_of(i), :]

        def work(h):
            gain = gain_ref[h]
            gain2 = gain * gain
            q = pick(qkv, h)
            k = pick(qkv, heads + h)
            v = pick(qkv, 2 * heads + h)
            cot = pick(cots, h)
            ecol = rates[:, rate_lane + h : rate_lane + h + 1]
            e = spread_lanes(ecol)
            e256 = spread_lanes(ecol, INNER)
            e3 = jnp.where(causal3, spread_lanes(ecol, 3 * MB), 0.0)
            khi, klo = hi_lo(k)
            qhi, qlo = hi_lo(q)
            left_k = rows2(khi, klo)
            qsplit = jnp.where(lane < HEAD, qhi.astype(F32), qlo.astype(F32)).astype(BF16)
            kq3 = fold(mm_nt(left_k, rows2(qsplit, qsplit, qsplit))) + 1.0
            yield
            pt3 = lanes3(e3 * kq3)
            ones = jnp.where(lane < HEAD + MB, 1.0, 0.0)
            qone = hi_lo(jnp.where(lane < HEAD, q, ones))
            kone = hi_lo(jnp.where(lane < HEAD, k, ones))
            left_q = jnp.transpose(rows2(stack3(*qone), stack3(*kone)))[: HEAD + MB]
            z1 = z1_ref[i, h]
            zq = zq_ref[i, h]
            m = m_ref[i, h]
            d2 = d2_ref[i, h]
            x = x_ref[i, h]
            y = y_ref[i, h]
            invq = rq_ref[i, h]
            act, slope, t, zs, sech, inner = gelu_parts(z1)
            curve = gelu_curve(z1, t, zs, sech, inner)
            qact, qslope = gelu_parts(zq)[:2]
            ahi, alo = hi_lo(act)
            qahi, qalo = hi_lo(qact)
            d1 = m * slope
            d1hi, d1lo = hi_lo(d1)
            d2hi, d2lo = hi_lo(d2)
            dy = gain * cot
            dy_mean = mean_dup(dy)
            dyy_mean = mean_dup(dy * y)
            yield
            dz2q = invq * (dy - dy_mean - y * dyy_mean)
            zhi, zlo = hi_lo(dz2q)
            dqa = fold(mm(rows2(zhi, zlo), s2_ref[i, h]))
            yield
            left_a = rows2(ahi, alo)
            aq3 = fold(mm_nt(left_a, rows2(qahi, qahi, qahi))) + mm_nt(ahi, rows2(qalo, qalo, qalo)) + 1.0
            yield
            zsplit = jnp.where(lane < HEAD, zhi.astype(F32), zlo.astype(F32)).astype(BF16)
            drt3 = -fold(mm_nt(rows2(d2hi, d2lo), rows2(zsplit, zsplit, zsplit)))
            yield
            rt3 = lanes3(e3 * aq3)
            dd2 = -mm(rt3, split3(zhi, zlo))
            de = jnp.sum(jnp.where(counted, drt3 * aq3, 0.0), axis=1, keepdims=True)
            du2t = e3 * drt3
            du2t_hi, du2t_lo = hi_lo(du2t[:, :MB])
            dqa = dqa + mm_tn(rows2(du2t_hi, du2t_lo, du2t_hi), split3(ahi, alo))
            yield
            da = mm(lanes3(du2t), split3(qahi, qalo))
            dzq = dqa * qslope
            zqhi, zqlo = hi_lo(dzq)
            dpt3 = -(fold(mm_nt(rows2(d1hi, d1lo), rows2(zqhi, zqhi, zqhi))) + mm_nt(d1hi, rows2(zqlo, zqlo, zqlo)))
            yield
            dd1 = -mm(pt3, split3(zqhi, zqlo))
            de = de + jnp.sum(jnp.where(counted, dpt3 * kq3, 0.0), axis=1, keepdims=True)
            du1t = e3 * dpt3
            du1t_hi, du1t_lo = hi_lo(du1t[:, :MB])
            dq = cot + mm_tn(rows2(du1t_hi, du1t_lo, du1t_hi), split3(khi, klo))
            dk = mm(lanes3(du1t), split3(qhi, qlo))
            yield
            left_2 = jnp.transpose(rows2(stack3(zhi, zlo), stack3(d2hi, d2lo)))[:HEAD]
            target = shift_ref[h] - v + k
            g = gain2 * x + gain * target
            put(
                refs, h, left_k, left_q, left_a, rows2(qahi, qalo), rows2(zqhi, zqlo), rows2(*hi_lo(e256 * d1)), rows2(*hi_lo(e * d2)), left_2,
                slope, m * curve, dd1, da,
                dd2, dq, dk, spread_lanes(de), dz2q, cot * y, cot, g, spread_lanes(mean_dup(g * x)), 2.0 * gain * x + target, e,
            )

        return [work(h) for h in range(heads)]

    def advance(i, refs, dqs, dks, dvs, des):
        following = resets_ref[jnp.minimum(block * steps + i + 1, resets_ref.shape[0] - 1)]
        carry_on = jnp.where(following == 1, 0.0, 1.0)

        def work(h):
            left_k, left_q, left_a, left_qa, left_zq, left_ed1, left_ed2, left_2, slope, mcurve, dd1, da, *rest = take(refs, h)
            dd2, dq, dk, de, dz2q, gain_part, cot, g, mgx, gain_factor, e = rest
            gain = gain_ref[h]
            gain2 = gain * gain
            s1 = s1_ref[i, h]
            s2 = s2_ref[i, h]
            m = m_ref[i, h]
            d2 = d2_ref[i, h]
            x = x_ref[i, h]
            inv = r_ref[i, h]
            w1f = w1[h] * carry_on
            w2f = w2[h] * carry_on
            b1v = b1[h] * carry_on
            b2v = b2[h] * carry_on
            w1s = rows2(*hi_lo(w1f))
            w2s = rows2(*hi_lo(w2f))
            de1 = -(fold(mm(left_k, w1s)) + b1v)
            yield
            e256 = jnp.concatenate([e, e], axis=1)
            dd1 = dd1 + e256 * de1
            dm = dd1 * slope
            dmhi, dmlo = hi_lo(dm)
            de2 = -(both_halves(fold(mm_nt(left_a, w2s))) + b2v)
            back = both_halves(fold(mm_nt(rows2(dmhi, dmlo), s2)))
            yield
            dd2 = dd2 + e * de2 + back
            yield
            q1 = mean_dup(dd2)
            q2 = mean_dup(dd2 * x)
            dr_r = mean_dup(dd2 * d2)
            yield
            dg = inv * (dd2 - q1 - x * q2)
            dx = dg * gain2 - inv * (dd2 * mgx + g * q2)
            x1 = mean_dup(dx)
            x2 = mean_dup(dx * x)
            yield
            dz2 = inv * (dx - x1 - x * x2) - x * inv * dr_r
            dz2hi, dz2lo = hi_lo(dz2)
            da = da - fold(mm(left_ed2, w2s)) + fold(mm(rows2(dz2hi, dz2lo), s2))
            yield
            dz1 = dd1 * mcurve + da * slope
            z1hi, z1lo = hi_lo(dz1)
            zqhi, zqlo = left_zq[:MB], left_zq[MB:]
            grads = mm(left_q, rows2(split3(zqhi, zqlo), split3(z1hi, z1lo)))
            yield
            w1[h] = w1f + grads[:HEAD]
            b1[h] = b1v + grads[HEAD:]
            ahi, alo = left_a[:MB], left_a[MB:]
            qahi, qalo = left_qa[:MB], left_qa[MB:]
            left_3 = jnp.transpose(stack3(dz2hi, dz2lo))[:HEAD]
            w2[h] = w2f + mm(left_2, rows2(split3(qahi, qalo), split3(dmhi, dmlo))) + mm(left_3, split3(ahi, alo))
            b2[h] = b2v + jnp.sum(dz2q + dz2, axis=0, keepdims=True)
            yield
            dkw = fold(mm_nt(left_ed1, w1s))
            to_rows = mm_nt(rows2(left_zq, z1hi, z1lo), s1)
            yield
            dgg = dg * gain
            dqs[h] = dq + both_halves(fold(to_rows[: 2 * MB]))
            dks[h] = dk + dgg + both_halves(fold(to_rows[2 * MB :]) - dkw)
            dvs[h] = -dgg
            des[h] = de[:, :1] + jnp.sum(m * slope * de1, axis=1, keepdims=True) + 0.5 * jnp.sum(d2 * de2, axis=1, keepdims=True)
            ggain[h] += gain_part + dg * gain_factor
            gshift[h] += cot + dgg

        return [work(h) for h in range(heads)]

    def step(i, now, later):
        dqs, dks, dvs, des = ([None] * heads for _ in range(4))
        interleave(advance(i, now, dqs, dks, dvs, des) + prepare(jnp.maximum(i - 1, 0), later))
        rates, sigs, _ = rates_at(i, qkv_ref[rows_of(i), :])
        dpre = jnp.zeros((MB, LANES), F32)
        for h in range(heads):
            dpre = jnp.where(lax.rem(lane, HEAD) == h, des[h], dpre)
        dqkv_ref[rows_of(i), :] = pack(dqs + dks + dvs + [dpre * rates * (1.0 - sigs)])

        @pl.when(resets_ref[block * steps + i] == 1)
        def _():
            gw1[...] += w1[...]
            gb1[...] += b1[...]
            gw2[...] += w2[...]
            gb2[...] += b2[...]

    interleave(prepare(steps - 1, ready[0]))

    def pair(at, carry):
        step(steps - 1 - 2 * at, ready[0], ready[1])
        step(steps - 2 - 2 * at, ready[1], ready[0])
        return carry

    lax.fori_loop(0, steps // 2, pair, 0)


def tiles_of(count):
    return -(-count // 2) * LANES


def state_scratch(heads):
    return [
        pltpu.VMEM((heads, HEAD, INNER), F32),
        pltpu.VMEM((heads, MB, INNER), F32),
        pltpu.VMEM((heads, HEAD, INNER), F32),
        pltpu.VMEM((heads, MB, LANES), F32),
    ]


def saved_shapes(total, heads):
    return [
        ((total, heads, LANES, INNER), BF16),
        ((total, heads, LANES, INNER), BF16),
        ((total, heads, MB, INNER), F32),
        ((total, heads, MB, INNER), F32),
        ((total, heads, MB, INNER), F32),
        ((total, heads, MB, LANES), F32),
        ((total, heads, MB, LANES), F32),
        ((total, heads, MB, LANES), F32),
        ((total, heads, MB, LANES), F32),
        ((total, heads, MB, LANES), F32),
    ]


def whole_spec(shape):
    zeros = (0,) * len(shape)
    return pl.BlockSpec(shape, lambda i, *_: zeros)


def chain_forward(resets, counts, cols, gate, bias, gain, shift, w1i, b1i, w2i, b2i, steps=8):
    heads = gain.shape[0]
    total = resets.shape[0]
    blocks = total // steps
    token_spec = lambda width: pl.BlockSpec((steps * MB, width), lambda i, *_: (i, 0))
    saved = saved_shapes(total, heads)
    saved_specs = [pl.BlockSpec((steps,) + s[1:], lambda i, *_: (i, 0, 0, 0)) for s, _ in saved]
    params = (bias, gain, shift, w1i, b1i, w2i, b2i)
    wide = tiles_of(heads)
    out = pl.pallas_call(
        functools.partial(fwd_kernel, heads, steps),
        grid_spec=pltpu.PrefetchScalarGridSpec(
            num_scalar_prefetch=2,
            grid=(blocks,),
            in_specs=[token_spec(cols.shape[1]), token_spec(wide)] + [whole_spec(p.shape) for p in params],
            out_specs=[token_spec(wide), token_spec(wide)] + saved_specs,
            scratch_shapes=state_scratch(heads) + 2 * fwd_ready(heads) + 2 * fwd_left(heads),
        ),
        out_shape=[jax.ShapeDtypeStruct((total * MB, wide), F32)] * 2 + [jax.ShapeDtypeStruct(s, d) for s, d in saved],
        compiler_params=pltpu.CompilerParams(dimension_semantics=("arbitrary",), vmem_limit_bytes=56 * 1024 * 1024),
        cost_estimate=pl.CostEstimate(flops=FWD_COST * total, bytes_accessed=1 << 20, transcendentals=0),
    )(resets, counts, cols, gate, *params)
    return out[0], out[1], out[2:]


def chain_backward(resets, counts, cols, bias, cot, gain, shift, saved, part=(0, 8), before=None, steps=8):
    heads = gain.shape[0]
    total = resets.shape[0]
    first = total // steps * part[0] // 8
    blocks = total // steps * part[1] // 8 - first
    last = first + blocks - 1
    token_spec = lambda width: pl.BlockSpec((steps * MB, width), lambda i, *_: (last - i, 0))
    wide = tiles_of(3 * heads + 1)
    saved_specs = [pl.BlockSpec((steps,) + s.shape[1:], lambda i, *_: (last - i, 0, 0, 0)) for s in saved]
    state_shapes = [(heads, HEAD, INNER), (heads, MB, INNER), (heads, HEAD, INNER), (heads, MB, LANES)]
    kept = state_shapes + state_shapes + [(heads, MB, LANES), (heads, MB, LANES)]
    kept_specs = [whole_spec(s) for s in kept]
    before = [] if before is None else list(before)
    out = pl.pallas_call(
        functools.partial(bwd_kernel, heads, steps, first, bool(before)),
        grid_spec=pltpu.PrefetchScalarGridSpec(
            num_scalar_prefetch=2,
            grid=(blocks,),
            in_specs=[token_spec(cols.shape[1]), whole_spec(bias.shape), token_spec(cot.shape[1]), whole_spec(gain.shape), whole_spec(shift.shape)]
            + saved_specs
            + kept_specs[: len(before)],
            out_specs=[pl.BlockSpec((steps * MB, wide), lambda i, *_: (blocks - 1 - i, 0))] + kept_specs,
            scratch_shapes=2 * bwd_ready(heads),
        ),
        out_shape=[jax.ShapeDtypeStruct((blocks * steps * MB, wide), F32)] + [jax.ShapeDtypeStruct(s, F32) for s in kept],
        compiler_params=pltpu.CompilerParams(dimension_semantics=("arbitrary",), vmem_limit_bytes=56 * 1024 * 1024),
        cost_estimate=pl.CostEstimate(flops=BWD_COST * blocks * steps, bytes_accessed=1 << 20, transcendentals=0),
    )(resets, counts, cols, bias, cot, gain, shift, *saved, *before)
    return out[0], out[1:]


HEADS = 12
high = lax.Precision.HIGH


def dot(left, right):
    return jnp.dot(left, right, precision=high)


def dot_t(left, right):
    return lax.dot_general(left, right, (((1,), (1,)), ((), ())), precision=high)


def t_dot(left, right):
    return lax.dot_general(left, right, (((0,), (0,)), ((), ())), precision=high)


def swap(value, axis, mask):
    count = lax.axis_size(axis)
    return lax.ppermute(value, axis, [(source, source ^ mask) for source in range(count)])


def bits_of(axis):
    count = lax.axis_size(axis)
    return [1 << at for at in reversed(range(count.bit_length() - 1))]


def upper_of(axis, mask):
    return (lax.axis_index(axis) & mask) != 0


def gather(value, axis, beside=None):
    shape = value.shape
    for done, mask in enumerate(bits_of(axis)):
        other = swap(value, axis, mask)
        if beside is not None and done == 0:
            other, beside = lax.optimization_barrier((other, beside))
        upper = upper_of(axis, mask)
        value = jnp.stack([jnp.where(upper, other, value), jnp.where(upper, value, other)], axis=done)
    value = value.reshape((-1,) + shape)
    return value if beside is None else (value, beside)


def gather_by_distance(value, axis):
    shape = value.shape
    for done, mask in enumerate(bits_of(axis)):
        value = jnp.stack([value, swap(value, axis, mask)], axis=done)
    return value.reshape((-1,) + shape)


def halves(value, axis, mask, dim):
    upper = upper_of(axis, mask)
    lower_half = lax.index_in_dim(value, 0, dim, keepdims=False)
    upper_half = lax.index_in_dim(value, 1, dim, keepdims=False)
    return jnp.where(upper, upper_half, lower_half), jnp.where(upper, lower_half, upper_half)


def row_stages(first=()):
    masks = bits_of("rows")
    order = [mask for mask in first if mask in masks] + [mask for mask in reversed(masks) if mask not in first]
    stages = []
    left = list(masks)
    for mask in order:
        stages.append(("rows", mask, left.index(mask)))
        left.remove(mask)
    return stages


def run_stages(value, stages):
    for axis, mask, dim in stages:
        keep, sent = halves(value, axis, mask, dim)
        value = keep + swap(sent, axis, mask)
    return value


def row_blocks(value):
    count = lax.axis_size("rows")
    return value.reshape((2,) * len(bits_of("rows")) + (value.shape[0] // count,) + value.shape[1:])


def low_bit_blocks(value, other=False):
    n = lax.axis_size("seq")
    share = value.shape[1] // n
    bit = (lax.axis_index("seq") & 1) ^ int(other)
    return jnp.stack([lax.dynamic_slice_in_dim(value, (2 * at + bit) * share, share, 1) for at in range(n // 2)])


def even_first(value):
    n = lax.axis_size("seq")
    share = value.shape[1] // n
    blocks = [value[:, at * share : (at + 1) * share] for at in list(range(0, n, 2)) + list(range(1, n, 2))]
    return jnp.concatenate(blocks, axis=1)


def own_half(value, other=False):
    share = value.shape[1] // 2
    bit = (lax.axis_index("seq") & 1) ^ int(other)
    return lax.dynamic_slice_in_dim(value, bit * share, share, 1)


def columns_to_tokens(value, width):
    n = lax.axis_size("seq")
    tokens = value.shape[0] // n
    moved = lax.all_to_all(value.reshape(n, tokens, -1), "seq", 0, 0)
    return moved.transpose(1, 0, 2).reshape(tokens, -1)[:, :width]


def tokens_to_columns(value):
    n = lax.axis_size("seq")
    tokens = value.shape[0]
    moved = lax.all_to_all(value.reshape(tokens, n, -1).transpose(1, 0, 2), "seq", 0, 0)
    return moved.reshape(n * tokens, -1)


def block_marks(lengths, total):
    block_counts = (lengths + MB - 1) // MB
    begins = (jnp.cumsum(block_counts, dtype=jnp.int32) - block_counts)[None, :]
    index = jnp.arange(total, dtype=jnp.int32)[:, None]
    resets = jnp.any(index == begins, axis=1).astype(jnp.int32)
    inside = jnp.clip(lengths[None, :] - MB * (index - begins), 0, MB)
    return resets, jnp.sum(jnp.where(index >= begins, inside, 0), axis=1)


def own_heads(value, axis, per_head, groups=1):
    n = lax.axis_size("seq")
    me = lax.axis_index("seq")
    count = -(-HEADS // n)
    shape = value.shape
    if n * count == HEADS:
        share = count * per_head
        parts = [lax.dynamic_slice_in_dim(value, g * HEADS * per_head + me * share, share, axis) for g in range(groups)]
        return jnp.concatenate(parts, axis=axis) if groups > 1 else parts[0]
    value = value.reshape(shape[:axis] + (groups, HEADS * per_head) + shape[axis + 1 :])
    pads = [(0, 0)] * value.ndim
    pads[axis + 1] = (0, (n * count - HEADS) * per_head)
    value = jnp.pad(value, pads)
    value = lax.dynamic_slice_in_dim(value, me * count * per_head, count * per_head, axis + 1)
    return value.reshape(shape[:axis] + (groups * count * per_head,) + shape[axis + 1 :])


def pad_columns(value, width):
    return jnp.pad(value, ((0, 0), (0, width - value.shape[1])))


def together(*values):
    return lax.optimization_barrier(values)


def local(
    layer_input,
    doc_lengths,
    output_grad,
    mixer_gain,
    triple_weight,
    rate_weight,
    rate_bias,
    first_weight,
    first_bias,
    second_weight,
    second_bias,
    inner_gain,
    inner_shift,
    gate_weight,
    output_weight,
    feed_gain,
    feed_weight,
    down_weight,
):
    n = lax.axis_size("seq")
    n_rows = lax.axis_size("rows")
    me = lax.axis_index("seq")
    heads = -(-HEADS // n)
    _, tokens, width = layer_input.shape
    span = tokens * n
    ff = down_weight.shape[0]
    head_cols = heads * HEAD
    x = layer_input[0]
    cot = output_grad[0]
    resets, counts = block_marks(doc_lengths[0], span // MB)

    inv = lax.rsqrt(jnp.mean(x * x, axis=-1, keepdims=True) + EPS)
    xhat = x * inv
    normed = xhat * mixer_gain
    split = tiles_of(3 * heads + 1)
    own_mixer = pad_columns(jnp.concatenate([own_heads(triple_weight, 1, HEAD, 3), own_heads(rate_weight, 1, 1)], axis=1), split)
    own_gate = pad_columns(own_heads(gate_weight, 1, HEAD), tiles_of(heads))
    rate_lane = HEAD * (3 * heads % 2)
    bias = jnp.broadcast_to(jnp.pad(own_heads(rate_bias, 0, 1), (rate_lane, LANES - heads - rate_lane))[None, :], (8, LANES))

    def per_head(value, rows, times):
        value = own_heads(value, 0, 1)
        return jnp.broadcast_to(jnp.concatenate([value] * times, axis=1)[:, None, :], (heads, rows, value.shape[1] * times))

    gain = per_head(inner_gain, MB, 2)
    shift = per_head(inner_shift, MB, 2)
    w1i = own_heads(first_weight, 0, 1)
    b1i = per_head(first_bias, MB, 1)
    w2t = own_heads(second_weight, 0, 1).transpose(0, 2, 1)
    w2i = w2t - jnp.mean(w2t, axis=1, keepdims=True)
    b2i = per_head(second_bias - jnp.mean(second_bias, axis=1, keepdims=True), MB, 2)
    normed_row, beside = gather(normed, "seq", (own_mixer, own_gate, bias, gain, shift, w1i, b1i, w2i, b2i, resets, counts))
    own_mixer, own_gate, bias, gain, shift, w1i, b1i, w2i, b2i, resets, counts = beside
    normed_row = normed_row.reshape(span, width)
    cols = jnp.dot(normed_row, own_mixer, precision=lax.Precision.HIGHEST)
    gate_pre = dot(normed_row, own_gate)
    gated_cols, mixed, saved = chain_forward(resets, counts, cols, gate_pre, bias, gain, shift, w1i, b1i, w2i, b2i)

    gated = columns_to_tokens(gated_cols[:, :head_cols], width)
    dhidden = dot_t(cot, down_weight)
    gated, dhidden = together(gated, dhidden)
    middle = x + dot(gated, output_weight)
    inv2 = lax.rsqrt(jnp.mean(middle * middle, axis=-1, keepdims=True) + EPS)
    mhat = middle * inv2
    second = mhat * feed_gain
    both = dot(second, feed_weight)
    left, right = both[:, :ff], both[:, ff:]
    sig = jax.nn.sigmoid(left)
    silu = left * sig
    hidden = silu * right
    narrow_stages = row_stages()
    cot_split = even_first(cot)
    down_sum = row_blocks(t_dot(hidden, own_half(cot_split)) + swap(t_dot(hidden, own_half(cot_split, True)), "seq", 1))
    down_keep, down_sent = halves(down_sum, *narrow_stages[0])
    down_other = swap(down_sent, *narrow_stages[0][:2])

    dboth = jnp.concatenate([dhidden * right * (sig + silu * (1.0 - sig)), dhidden * silu], axis=1)
    dsecond = dot_t(dboth, feed_weight)
    feed_gain_part = jnp.sum(dsecond * mhat, axis=0)
    dmhat = dsecond * feed_gain
    dmiddle = cot + inv2 * (dmhat - mhat * jnp.mean(dmhat * mhat, axis=-1, keepdims=True))
    dgated = tokens_to_columns(pad_columns(dot_t(dmiddle, output_weight), n * head_cols))

    second_row = gather_by_distance(second, "seq").reshape(span, width)
    feed_moved = jnp.stack([low_bit_blocks(dboth), swap(low_bit_blocks(dboth, True), "seq", 1)], axis=1)
    dmiddle_split = even_first(dmiddle)
    output_sum = row_blocks(t_dot(gated, own_half(dmiddle_split)) + swap(t_dot(gated, own_half(dmiddle_split, True)), "seq", 1))
    output_keep, output_sent = halves(output_sum, *narrow_stages[0])
    feed_masks = bits_of("seq")[:-1]
    feed_moved = feed_moved.reshape((2,) * len(feed_masks) + (2, tokens, -1))
    for mask in feed_masks[:0:-1]:
        keep, sent = halves(feed_moved, "seq", mask, feed_masks.index(mask))
        feed_moved = jnp.stack([keep, swap(sent, "seq", mask)], axis=feed_masks.index(mask))
        feed_moved = feed_moved.reshape(feed_moved.shape[: feed_masks.index(mask)] + (-1, tokens, feed_moved.shape[-1]))
    feed_keep, feed_sent = halves(feed_moved, "seq", feed_masks[0], 0)
    dgated, output_sent, feed_sent = together(dgated, output_sent, feed_sent)
    feed_other = swap(feed_sent, "seq", feed_masks[0])
    output_other = swap(output_sent, *narrow_stages[0][:2])

    dgated = dgated[:, :head_cols]
    gate_act, gate_slope = gelu_parts(gate_pre[:, :head_cols])[:2]
    dmixed = pad_columns(dgated * gate_act, tiles_of(heads))
    dgate = dgated * mixed[:, :head_cols] * gate_slope
    backward = functools.partial(chain_backward, resets, counts, cols, bias, dmixed, gain, shift, saved)
    part_a, kept = backward(part=(5, 8))

    part_a, kept, down_other, output_other, feed_other, dgate = together(part_a, kept, down_other, output_other, feed_other, dgate)
    dboth_row = jnp.stack([feed_keep, feed_other]).reshape(span, -1)
    feed_cols = dboth_row.shape[1]
    gate_part = t_dot(normed_row, dgate)
    feed = row_blocks(jnp.concatenate([t_dot(second_row, dboth_row), gate_part], axis=1))
    dnormed_gate = dot_t(dgate, own_gate[:, :head_cols])
    feed_stages = row_stages()
    feed_keep, feed_sent = halves(feed, *feed_stages[0])
    narrow = jnp.concatenate([down_keep + down_other, output_keep + output_other], axis=-2)
    narrow_keep, narrow_sent = halves(narrow, *narrow_stages[1])
    kept, feed_sent, narrow_sent, dnormed_gate = together(kept, feed_sent, narrow_sent, dnormed_gate)
    feed_other = swap(feed_sent, *feed_stages[0][:2])
    narrow_other = swap(narrow_sent, *narrow_stages[1][:2])
    part_b, kept = backward(part=(2, 5), before=kept)
    part_b, hidden, middle = together(part_b, hidden, middle)
    layer_output = middle + dot(hidden, down_weight)

    part_b, kept, narrow_other, feed_other = together(part_b, kept, narrow_other, feed_other)
    feed_keep, feed_sent = halves(feed_keep + feed_other, *feed_stages[1])
    narrow_keep, narrow_sent = halves(narrow_keep + narrow_other, *narrow_stages[2])
    kept, feed_sent, narrow_sent = together(kept, feed_sent, narrow_sent)
    feed_other = swap(feed_sent, *feed_stages[1][:2])
    narrow_other = swap(narrow_sent, *narrow_stages[2][:2])
    part_c, kept = backward(part=(0, 2), before=kept)

    part_c, kept, narrow_other, feed_other = together(part_c, kept, narrow_other, feed_other)
    feed = run_stages(feed_keep + feed_other, feed_stages[2:])
    narrow = run_stages(narrow_keep + narrow_other, narrow_stages[3:])
    seq_masks = bits_of("seq")[:-1]
    narrow = jnp.stack(jnp.split(narrow, n // 2, axis=1)).reshape((2,) * len(seq_masks) + (narrow.shape[0], -1))
    narrow = run_stages(narrow, [("seq", mask, seq_masks.index(mask)) for mask in reversed(seq_masks)])
    down_weight_grad, output_weight_grad = narrow[: ff // n_rows], narrow[ff // n_rows :]
    feed_weight_grad, gate_weight_grad = feed[:, :feed_cols], feed[:, feed_cols:]

    dcols = jnp.concatenate([part_c, part_b, part_a])
    triple_part = t_dot(normed_row, dcols)
    triple_blocks = row_blocks(triple_part)
    triple_sum = run_stages(triple_blocks, row_stages())
    dcols, triple_part = together(dcols, triple_part)
    dnormed = dot_t(dcols, own_mixer) + dnormed_gate
    dnormed = dnormed.reshape((2,) * len(bits_of("seq")) + (tokens, width))
    seq_order = [("seq", mask, bits_of("seq").index(mask)) for mask in reversed(bits_of("seq"))]
    dnormed = run_stages(dnormed, seq_order[:-1])
    dnormed_keep, dnormed_sent = halves(dnormed, *seq_order[-1])

    rate_tile = dcols[:, 3 * head_cols - rate_lane :][:, :LANES]
    rate_part = t_dot(rate_tile, normed_row)[rate_lane : rate_lane + heads]
    mixer_gain_part = jnp.sum(triple_part * own_mixer, axis=1)
    mixer_gain_part = (mixer_gain_part + jnp.sum(gate_part * own_gate[:, :head_cols], axis=1)) / mixer_gain
    gw1, gb1, gw2, gb2, ggain, gshift = kept[4:]
    lane_sums = jnp.sum(rate_tile, axis=0)[rate_lane : rate_lane + heads]
    narrow_rows = jnp.concatenate(
        [gb2[:, 0, :HEAD], jnp.sum(ggain, axis=1)[:, :HEAD], jnp.sum(gshift, axis=1)[:, :HEAD], lane_sums[:, None]], axis=1
    )
    pieces = [
        gw1.reshape(-1, INNER),
        gw2.reshape(-1, INNER),
        gb1[:, 0],
        pad_columns(narrow_rows, INNER),
        rate_part.reshape(-1, INNER),
        jnp.stack([mixer_gain_part, feed_gain_part]).reshape(-1, INNER),
    ]
    lengths = [piece.shape[0] for piece in pieces]
    rest = jnp.concatenate(pieces[2:])
    rest = jnp.pad(rest, ((0, -sum(lengths) % (n_rows * 8)), (0, 0)))
    small = jnp.concatenate(pieces[:2] + [rest])
    small, dnormed_sent = together(small, dnormed_sent)
    dnormed_other = swap(dnormed_sent, *seq_order[-1][:2])
    small = run_stages(row_blocks(small), row_stages())
    small = gather(small, "rows")
    small, dnormed_other = together(small, dnormed_other)
    small = gather(small, "seq").reshape(n, -1, INNER)
    starts = [sum(lengths[:at]) for at in range(len(lengths))]
    small = [small[:, start : start + length] for start, length in zip(starts, lengths)]
    first_weight_grad = small[0].reshape(n * heads, HEAD, INNER)[:HEADS]
    second_weight_grad = small[1].reshape(n * heads, HEAD, INNER)[:HEADS].transpose(0, 2, 1)
    first_bias_grad = small[2].reshape(n * heads, INNER)[:HEADS]
    narrow_rows = small[3].reshape(n * heads, INNER)[:HEADS]
    second_bias_grad, inner_gain_grad, inner_shift_grad = (narrow_rows[:, HEAD * at : HEAD * (at + 1)] for at in range(3))
    rate_bias_grad = narrow_rows[:, 3 * HEAD]
    rate_weight_grad = small[4].reshape(n * heads, width)[:HEADS].T
    gains = jnp.sum(small[5], axis=0).reshape(2, width)

    dxhat = (dnormed_keep + dnormed_other) * mixer_gain
    input_grad = dmiddle + inv * (dxhat - xhat * jnp.mean(dxhat * xhat, axis=-1, keepdims=True))

    triple_every = gather(triple_sum, "seq")
    share = 3 * width // n
    if n * heads == HEADS and share % head_cols == 0:
        blocks = []
        for at in range(share // head_cols):
            block = me * (share // head_cols) + at
            columns = lax.dynamic_slice(triple_every, (block % n, 0, block // n * head_cols), (1, triple_every.shape[1], head_cols))
            blocks.append(columns[0])
        triple_weight_grad = jnp.concatenate(blocks, axis=1)
    else:
        every = triple_every[:, :, : 3 * head_cols].reshape(n, -1, 3, head_cols).transpose(1, 2, 0, 3)
        every = every.reshape(every.shape[0], 3, -1)[:, :, :width].reshape(every.shape[0], 3 * width)
        triple_weight_grad = lax.dynamic_slice_in_dim(every, me * share, share, 1)
    if n * heads != HEADS:
        every = gather(gate_weight_grad, "seq").transpose(1, 0, 2)
        every = every.reshape(every.shape[0], -1)[:, :width]
        gate_weight_grad = lax.dynamic_slice_in_dim(every, me * (width // n), width // n, 1)

    return (
        layer_output[None],
        input_grad[None],
        gains[0],
        triple_weight_grad,
        rate_weight_grad,
        rate_bias_grad,
        first_weight_grad,
        first_bias_grad,
        second_weight_grad,
        second_bias_grad,
        inner_gain_grad,
        inner_shift_grad,
        gate_weight_grad,
        output_weight_grad,
        gains[1],
        feed_weight_grad,
        down_weight_grad,
    )


def solution(mesh):
    tokens = P("rows", "seq", None)
    shard = P("rows", "seq")
    in_specs = (tokens, P("rows", None), tokens) + (P(),) * 15
    out_specs = (tokens, tokens, P(), shard) + (P(),) * 8 + (shard, shard, P(), shard, shard)
    return jax.shard_map(local, mesh=mesh, in_specs=in_specs, out_specs=out_specs, check_vma=False)
```

```python
import functools
import jax
import jax.numpy as jnp
from jax import lax
from jax.experimental import pallas as pl
from jax.experimental.pallas import tpu as pltpu
from jax.sharding import PartitionSpec as P

HEAD = 64
INNER = 256
MB = 16
EPS = 1e-06
RTP = 0.7978845608028654
F32 = jnp.float32
BF16 = jnp.bfloat16
LANES = 128
BASE_RATE = 0.1
FWD_COST = 1_500_000_000
BWD_COST = 2_000_000_000


def hi_lo(value):
    high = value.astype(BF16)
    return high, (value - high.astype(F32)).astype(BF16)


def hi_mid_lo(value):
    high = value.astype(BF16)
    rest = value - high.astype(F32)
    mid = rest.astype(BF16)
    return high, mid, (rest - mid.astype(F32)).astype(BF16)


def fold_all(value):
    total = value[:MB]
    for at in range(MB, value.shape[0], MB):
        total = total + value[at : at + MB]
    return total


def six_left(high, mid, low):
    return rows2(high, high, high, mid, mid, low)


def six_right(high, mid, low):
    return rows2(high, mid, low, high, mid, high)


def three_times(value):
    return jnp.concatenate([value, value[:, :HEAD]], axis=1)


def mm(left, right):
    return lax.dot_general(left, right, (((1,), (0,)), ((), ())), preferred_element_type=F32)


def mm_nt(left, right):
    return lax.dot_general(left, right, (((1,), (1,)), ((), ())), preferred_element_type=F32)


def mm_tn(left, right):
    return lax.dot_general(left, right, (((0,), (0,)), ((), ())), preferred_element_type=F32)


def rows2(*parts):
    return jnp.concatenate(parts, axis=0)


def fold(value):
    return value[:MB] + value[MB:]


def half_turn(value):
    return pltpu.roll(value, HEAD, 1)


def both_halves(value):
    return value + half_turn(value)


def lane_of(shape):
    return lax.broadcasted_iota(jnp.int32, shape, 1)


def pick(block, unit):
    tile = block[:, (unit // 2) * LANES : (unit // 2 + 1) * LANES]
    turned = half_turn(tile)
    low_half = lane_of(tile.shape) < HEAD
    if unit % 2 == 0:
        return jnp.where(low_half, tile, turned)
    return jnp.where(low_half, turned, tile)


def pack(parts):
    tiles = []
    for at in range(0, len(parts), 2):
        left = parts[at]
        right = parts[at + 1] if at + 1 < len(parts) else jnp.zeros_like(left)
        tiles.append(jnp.where(lane_of(left.shape) < HEAD, left, right))
    return jnp.concatenate(tiles, axis=1) if len(tiles) > 1 else tiles[0]


def mean_dup(value):
    return jnp.sum(value, axis=1, keepdims=True) * (1.0 / LANES)


def gelu_parts(z):
    z2 = z * z
    t = jnp.tanh(z * (RTP + (RTP * 0.044715) * z2))
    one_t = 0.5 + 0.5 * t
    sech = (1.0 - t) * one_t
    inner = RTP + (RTP * 0.134145) * z2
    act = z * one_t
    zs = z * sech
    slope = one_t + zs * inner
    return act, slope, t, zs, sech, inner


def gelu_curve(z, t, zs, sech, inner):
    return 2.0 * sech * inner + zs * ((2.0 * RTP * 0.134145) * z) - 2.0 * t * zs * inner * inner


def split3(high, low):
    return rows2(high, high, low)


def stack3(high, low):
    return rows2(high, low, high)


def lanes3(value):
    high, low = hi_lo(value)
    lane = lane_of(value.shape)
    return jnp.where((lane >= MB) & (lane < 2 * MB), low.astype(F32), high.astype(F32)).astype(BF16)


def interleave(works):
    works = list(works)
    while works:
        for work in list(works):
            try:
                next(work)
            except StopIteration:
                works.remove(work)


def rates_of(cols, bias_ref, heads, count):
    unit = 3 * heads
    tile = cols[:, (unit // 2) * LANES : (unit // 2 + 1) * LANES] + bias_ref[:1]
    sig = 0.5 + 0.5 * jnp.tanh(0.5 * tile)
    row = lax.broadcasted_iota(jnp.int32, tile.shape, 0)
    return jnp.where(row < count, (BASE_RATE / HEAD) * sig, 0.0), sig, HEAD * (unit % 2)


def put(refs, head, *values):
    for ref, value in zip(refs, values, strict=True):
        ref[head] = value


def take(refs, head):
    return [ref[head] for ref in refs]


def spread_lanes(column, width=LANES):
    return jnp.broadcast_to(column, (MB, width))


def fwd_ready(heads):
    shapes = [((5 * MB, 3 * HEAD), BF16), ((HEAD + 2 * MB, 3 * MB), BF16), ((MB, 3 * MB), F32)] + [((MB, LANES), F32)] * 4
    return [pltpu.VMEM((heads,) + shape, dtype) for shape, dtype in shapes]


def fwd_left(heads):
    shapes = [((2 * MB, INNER), BF16), ((2 * MB, LANES), BF16), ((MB, 3 * MB), F32), ((MB, LANES), F32), ((MB, LANES), F32)]
    return [pltpu.VMEM((heads,) + shape, dtype) for shape, dtype in shapes]


def fwd_kernel(heads, steps, resets_ref, counts_ref, qkv_ref, gate_ref, bias_ref, gain_ref, shift_ref, w1i, b1i, w2i, b2i,
               gated_ref, mixed_ref, s1_ref, s2_ref, z1_ref, zq_ref, m_ref, d2_ref, x_ref, y_ref, r_ref, rq_ref,
               w1, b1, w2, b2, *ready):
    block = pl.program_id(0)
    count = len(fwd_ready(heads))
    ready, left = (ready[:count], ready[count : 2 * count]), ready[2 * count :]
    left = (left[: len(left) // 2], left[len(left) // 2 :])
    lane = lane_of((MB, LANES))
    row = lax.broadcasted_iota(jnp.int32, (MB, LANES), 0)
    lane48 = lane_of((MB, 3 * MB))
    row48 = lax.broadcasted_iota(jnp.int32, (MB, 3 * MB), 0)
    causal = (lane >= HEAD) & (lane < HEAD + MB) & (row <= lane - HEAD)

    def rows_of(i):
        return pl.ds(pl.multiple_of(i * MB, MB), MB)

    def prepare(i, refs):
        qkv = qkv_ref[rows_of(i), :]
        rates, _, rate_lane = rates_of(qkv, bias_ref, heads, counts_ref[block * steps + i])

        def work(h):
            q = pick(qkv, h)
            k = pick(qkv, heads + h)
            v = pick(qkv, 2 * heads + h)
            e = spread_lanes(rates[:, rate_lane + h : rate_lane + h + 1])
            yield
            coef = gain_ref[h] * (shift_ref[h] - v + k)
            khi, klo = hi_lo(k)
            qhi, qlo = hi_lo(q)
            left_a = three_times(rows2(*hi_mid_lo(k), qhi, qlo))
            qsplit = jnp.where(lane < HEAD, qhi.astype(F32), qlo.astype(F32)).astype(BF16)
            zero = jnp.zeros((HEAD, LANES), BF16)
            kq = fold(mm_nt(rows2(khi, klo), rows2(zero, qsplit, zero[: HEAD - MB])))
            yield
            left_d = e * jnp.where(lane < HEAD, k, jnp.where(causal, kq + 1.0, jnp.where((lane >= HEAD + MB) & (lane < HEAD + 2 * MB), 1.0, 0.0)))
            left_d3 = jnp.transpose(stack3(*hi_lo(left_d)))[: HEAD + 2 * MB]
            erow = jnp.transpose(e)[:MB, :]
            e3 = jnp.where(lax.rem(lane48, MB) <= row48, jnp.concatenate([erow, erow, erow], axis=1), 0.0)
            yield
            put(refs, h, left_a, left_d3, e3, e, q, coef, spread_lanes(mean_dup(coef)))

        return [work(h) for h in range(heads)]

    def advance(i, refs, left):
        def work(h):
            left_a, left_d3, e3, e, q, coef, coef_mean = take(refs, h)
            gain = gain_ref[h]
            gain2 = gain * gain
            w1f = w1[h]
            w2f = w2[h]
            w1s = rows2(*hi_mid_lo(w1f))
            w2hi, w2mid, w2lo = hi_mid_lo(w2f)
            w2s = rows2(w2hi, w2mid)
            s1_ref[i, h] = w1s[: 2 * HEAD]
            s2_ref[i, h] = w2s
            b1v = b1[h]
            b2v = b2[h]
            z = mm(left_a, w1s)
            yield
            z1 = fold_all(z[: 3 * MB]) + b1v
            act, slope = gelu_parts(z1)[:2]
            ahi, alo, arest = hi_mid_lo(act)
            z2 = fold_all(mm_nt(rows2(ahi, alo, arest), rows2(w2s, w2lo, jnp.zeros((HEAD, INNER), BF16))))
            yield
            z2 = both_halves(z2[:, :LANES] + z2[:, LANES:]) + b2v
            yield
            g2z = gain2 * z2
            inv = lax.rsqrt(mean_dup(z2 * z2) + EPS)
            m1 = mean_dup(g2z)
            m2 = mean_dup(g2z * z2)
            m3 = mean_dup(coef * z2)
            yield
            x = z2 * inv
            g = gain2 * x + coef
            d2 = inv * (g - (inv * m1 + coef_mean) - x * (inv * inv * m2 + inv * m3))
            d2hi, d2lo = hi_lo(d2)
            m = fold(mm(rows2(d2hi, d2lo), w2s))
            yield
            d1 = m * slope
            u = mm(left_d3, split3(*hi_lo(d1)))
            yield
            w1[h] = w1f - u[:HEAD]
            b1[h] = b1v - u[HEAD + MB :]
            ed2 = e * d2
            w2[h] = w2f - mm(jnp.transpose(six_left(*hi_mid_lo(ed2)))[:HEAD], six_right(ahi, alo, arest))
            b2[h] = b2v - jnp.sum(ed2, axis=0, keepdims=True)
            z1_ref[i, h] = z1
            zq_ref[i, h] = fold(z[3 * MB :]) + b1v - u[HEAD : HEAD + MB]
            m_ref[i, h] = m
            d2_ref[i, h] = d2
            x_ref[i, h] = x
            r_ref[i, h] = spread_lanes(inv)
            put(left, h, rows2(ahi, alo), rows2(d2hi, d2lo), e3, q, b2v)

        return [work(h) for h in range(heads)]

    def finish(i, left, outs):
        def work(h):
            left_b, left_c, e3, q, b2v = take(left, h)
            ahi, alo = left_b[:MB], left_b[MB:]
            w2s = s2_ref[i, h]
            qact = gelu_parts(zq_ref[i, h])[0]
            qahi, qalo = hi_lo(qact)
            left_e = rows2(qahi, qalo)
            uq = fold(mm_nt(left_e, rows2(ahi, ahi, ahi))) + mm_nt(qahi, rows2(alo, alo, alo))
            z2q = fold(mm_nt(left_e, w2s))
            yield
            r3 = lanes3(e3 * (uq + 1.0))
            z2q = both_halves(z2q) + b2v - mm(r3, split3(left_c[:MB], left_c[MB:]))
            yield
            invq = lax.rsqrt(mean_dup(z2q * z2q) + EPS)
            yield
            y = z2q * invq
            outs[h] = q + gain_ref[h] * y + shift_ref[h]
            y_ref[i, h] = y
            rq_ref[i, h] = spread_lanes(invq)

        return [work(h) for h in range(heads)]

    def store(i, outs):
        mixed = pack(outs)
        mixed_ref[rows_of(i), :] = mixed
        gated_ref[rows_of(i), :] = gelu_parts(gate_ref[rows_of(i), :])[0] * mixed

    def step(i, now, later, parity):
        @pl.when(resets_ref[block * steps + i] == 1)
        def _():
            w1[...] = w1i[...]
            b1[...] = jnp.broadcast_to(b1i[...], b1.shape)
            w2[...] = w2i[...]
            b2[...] = jnp.broadcast_to(b2i[...], b2.shape)

        outs = [None] * heads
        behind = jnp.maximum(i - 1, 0)
        interleave(advance(i, now, left[parity]) + finish(behind, left[1 - parity], outs) + prepare(jnp.minimum(i + 1, steps - 1), later))
        store(behind, outs)

    interleave(prepare(0, ready[0]))

    def pair(at, carry):
        step(2 * at, ready[0], ready[1], 0)
        step(2 * at + 1, ready[1], ready[0], 1)
        return carry

    lax.fori_loop(0, steps // 2, pair, 0)
    outs = [None] * heads
    interleave(finish(steps - 1, left[1], outs))
    store(steps - 1, outs)


def bwd_ready(heads):
    halves = [(2 * MB, LANES), (HEAD + MB, 6 * MB), (2 * MB, INNER), (2 * MB, INNER), (2 * MB, INNER), (2 * MB, INNER), (2 * MB, LANES), (HEAD, 6 * MB)]
    wide = [(MB, INNER)] * 4
    rest = [(MB, LANES)] * 11
    shapes = [(shape, BF16) for shape in halves] + [(shape, F32) for shape in wide + rest]
    return [pltpu.VMEM((heads,) + shape, dtype) for shape, dtype in shapes]


def bwd_left(heads):
    shapes = [((LANES, INNER), BF16), ((4 * MB, INNER), BF16), ((2 * MB, INNER), BF16)] + [((MB, LANES), F32)] * 5
    return [pltpu.VMEM((heads,) + shape, dtype) for shape, dtype in shapes]


def bwd_kernel(heads, steps, first_block, begun, resets_ref, counts_ref, qkv_ref, bias_ref, cot_ref, gain_ref, shift_ref,
               s1_ref, s2_ref, z1_ref, zq_ref, m_ref, d2_ref, x_ref, y_ref, r_ref, rq_ref, *refs):
    before = refs[:10] if begun else None
    dqkv_ref, w1, b1, w2, b2, gw1, gb1, gw2, gb2, ggain, gshift, *ready = refs[10 if begun else 0 :]
    count = len(bwd_ready(heads))
    ready, left = (ready[:count], ready[count : 2 * count]), ready[2 * count :]
    left = (left[: len(left) // 2], left[len(left) // 2 :])
    blocks = pl.num_programs(0)
    block = first_block + blocks - 1 - pl.program_id(0)
    lane = lane_of((MB, LANES))
    lane48 = lane_of((MB, 3 * MB))
    row48 = lax.broadcasted_iota(jnp.int32, (MB, 3 * MB), 0)
    causal3 = row48 <= lax.rem(lane48, MB)
    counted = causal3 & (lane48 < MB)

    @pl.when(pl.program_id(0) == 0)
    def _():
        for at, ref in enumerate((w1, b1, w2, b2, gw1, gb1, gw2, gb2, ggain, gshift)):
            ref[...] = before[at][...] if begun else jnp.zeros_like(ref)

    def rows_of(i):
        return pl.ds(pl.multiple_of(i * MB, MB), MB)

    def rates_at(i, qkv):
        return rates_of(qkv, bias_ref, heads, counts_ref[block * steps + i])

    def prepare(i, refs):
        qkv = qkv_ref[rows_of(i), :]
        rates, sigs, rate_lane = rates_at(i, qkv)
        cots = cot_ref[rows_of(i), :]

        def work(h):
            gain = gain_ref[h]
            gain2 = gain * gain
            q = pick(qkv, h)
            k = pick(qkv, heads + h)
            v = pick(qkv, 2 * heads + h)
            cot = pick(cots, h)
            ecol = rates[:, rate_lane + h : rate_lane + h + 1]
            e = spread_lanes(ecol)
            e256 = spread_lanes(ecol, INNER)
            e3 = jnp.where(causal3, spread_lanes(ecol, 3 * MB), 0.0)
            khi, klo = hi_lo(k)
            qhi, qlo = hi_lo(q)
            left_k = rows2(khi, klo)
            qsplit = jnp.where(lane < HEAD, qhi.astype(F32), qlo.astype(F32)).astype(BF16)
            kq3 = fold(mm_nt(left_k, rows2(qsplit, qsplit, qsplit))) + 1.0
            yield
            pt3 = lanes3(e3 * kq3)
            ones = jnp.where(lane < HEAD + MB, 1.0, 0.0)
            qone = hi_lo(jnp.where(lane < HEAD, q, ones))
            kone = hi_lo(jnp.where(lane < HEAD, k, ones))
            left_q = jnp.transpose(rows2(stack3(*qone), stack3(*kone)))[: HEAD + MB]
            z1 = z1_ref[i, h]
            zq = zq_ref[i, h]
            m = m_ref[i, h]
            d2 = d2_ref[i, h]
            x = x_ref[i, h]
            y = y_ref[i, h]
            invq = rq_ref[i, h]
            act, slope, t, zs, sech, inner = gelu_parts(z1)
            curve = gelu_curve(z1, t, zs, sech, inner)
            qact, qslope = gelu_parts(zq)[:2]
            ahi, alo = hi_lo(act)
            qahi, qalo = hi_lo(qact)
            d1 = m * slope
            d1hi, d1lo = hi_lo(d1)
            d2hi, d2lo = hi_lo(d2)
            dy = gain * cot
            dy_mean = mean_dup(dy)
            dyy_mean = mean_dup(dy * y)
            yield
            dz2q = invq * (dy - dy_mean - y * dyy_mean)
            zhi, zlo = hi_lo(dz2q)
            dqa = fold(mm(rows2(zhi, zlo), s2_ref[i, h]))
            yield
            left_a = rows2(ahi, alo)
            aq3 = fold(mm_nt(left_a, rows2(qahi, qahi, qahi))) + mm_nt(ahi, rows2(qalo, qalo, qalo)) + 1.0
            yield
            zsplit = jnp.where(lane < HEAD, zhi.astype(F32), zlo.astype(F32)).astype(BF16)
            drt3 = -fold(mm_nt(rows2(d2hi, d2lo), rows2(zsplit, zsplit, zsplit)))
            yield
            rt3 = lanes3(e3 * aq3)
            dd2 = -mm(rt3, split3(zhi, zlo))
            de = jnp.sum(jnp.where(counted, drt3 * aq3, 0.0), axis=1, keepdims=True)
            du2t = e3 * drt3
            du2t_hi, du2t_lo = hi_lo(du2t[:, :MB])
            dqa = dqa + mm_tn(rows2(du2t_hi, du2t_lo, du2t_hi), split3(ahi, alo))
            yield
            da = mm(lanes3(du2t), split3(qahi, qalo))
            dzq = dqa * qslope
            zqhi, zqlo = hi_lo(dzq)
            dpt3 = -(fold(mm_nt(rows2(d1hi, d1lo), rows2(zqhi, zqhi, zqhi))) + mm_nt(d1hi, rows2(zqlo, zqlo, zqlo)))
            yield
            dd1 = -mm(pt3, split3(zqhi, zqlo))
            de = de + jnp.sum(jnp.where(counted, dpt3 * kq3, 0.0), axis=1, keepdims=True)
            du1t = e3 * dpt3
            du1t_hi, du1t_lo = hi_lo(du1t[:, :MB])
            dq = cot + mm_tn(rows2(du1t_hi, du1t_lo, du1t_hi), split3(khi, klo))
            dk = mm(lanes3(du1t), split3(qhi, qlo))
            yield
            left_2 = jnp.transpose(rows2(stack3(zhi, zlo), stack3(d2hi, d2lo)))[:HEAD]
            target = shift_ref[h] - v + k
            g = gain2 * x + gain * target
            put(
                refs, h, left_k, left_q, left_a, rows2(qahi, qalo), rows2(zqhi, zqlo), rows2(*hi_lo(e256 * d1)), rows2(*hi_lo(e * d2)), left_2,
                slope, m * curve, dd1, da,
                dd2, dq, dk, spread_lanes(de), dz2q, cot * y, cot, g, spread_lanes(mean_dup(g * x)), 2.0 * gain * x + target, e,
            )

        return [work(h) for h in range(heads)]

    def advance(i, refs, left):
        following = resets_ref[jnp.minimum(block * steps + i + 1, resets_ref.shape[0] - 1)]
        carry_on = jnp.where(following == 1, 0.0, 1.0)

        def work(h):
            left_k, left_q, left_a, left_qa, left_zq, left_ed1, left_ed2, left_2, slope, mcurve, dd1, da, *rest = take(refs, h)
            dd2, dq, dk, de, dz2q, gain_part, cot, g, mgx, gain_factor, e = rest
            gain = gain_ref[h]
            gain2 = gain * gain
            s2 = s2_ref[i, h]
            m = m_ref[i, h]
            d2 = d2_ref[i, h]
            x = x_ref[i, h]
            inv = r_ref[i, h]
            w1f = w1[h] * carry_on
            w2f = w2[h] * carry_on
            b1v = b1[h] * carry_on
            b2v = b2[h] * carry_on
            w1s = rows2(*hi_lo(w1f))
            w2s = rows2(*hi_lo(w2f))
            de1 = -(fold(mm(left_k, w1s)) + b1v)
            yield
            e256 = jnp.concatenate([e, e], axis=1)
            dd1 = dd1 + e256 * de1
            dm = dd1 * slope
            dmhi, dmlo = hi_lo(dm)
            de2 = -(both_halves(fold(mm_nt(left_a, w2s))) + b2v)
            back = both_halves(fold(mm_nt(rows2(dmhi, dmlo), s2)))
            yield
            dd2 = dd2 + e * de2 + back
            yield
            q1 = mean_dup(dd2)
            q2 = mean_dup(dd2 * x)
            dr_r = mean_dup(dd2 * d2)
            yield
            dg = inv * (dd2 - q1 - x * q2)
            dx = dg * gain2 - inv * (dd2 * mgx + g * q2)
            x1 = mean_dup(dx)
            x2 = mean_dup(dx * x)
            yield
            dz2 = inv * (dx - x1 - x * x2) - x * inv * dr_r
            dz2hi, dz2lo = hi_lo(dz2)
            da = da - fold(mm(left_ed2, w2s)) + fold(mm(rows2(dz2hi, dz2lo), s2))
            yield
            dz1 = dd1 * mcurve + da * slope
            z1hi, z1lo = hi_lo(dz1)
            zqhi, zqlo = left_zq[:MB], left_zq[MB:]
            grads = mm(left_q, rows2(split3(zqhi, zqlo), split3(z1hi, z1lo)))
            yield
            w1[h] = w1f + grads[:HEAD]
            b1[h] = b1v + grads[HEAD:]
            ahi, alo = left_a[:MB], left_a[MB:]
            qahi, qalo = left_qa[:MB], left_qa[MB:]
            left_3 = jnp.transpose(stack3(dz2hi, dz2lo))[:HEAD]
            w2[h] = w2f + mm(left_2, rows2(split3(qahi, qalo), split3(dmhi, dmlo))) + mm(left_3, split3(ahi, alo))
            b2[h] = b2v + jnp.sum(dz2q + dz2, axis=0, keepdims=True)
            dgg = dg * gain
            rate_terms = m * slope * de1
            rate_terms = rate_terms[:, :LANES] + rate_terms[:, LANES:] + 0.5 * (d2 * de2)
            ggain[h] += gain_part + dg * gain_factor
            gshift[h] += cot + dgg
            put(left, h, w1s, rows2(left_zq, z1hi, z1lo), left_ed1, dq, dk + dgg, -dgg, de, rate_terms)

        return [work(h) for h in range(heads)]

    def finish(i, left, dqs, dks, dvs, des):
        def work(h):
            w1s, left_z, left_ed1, dq, dk, dv, de, rate_terms = take(left, h)
            dkw = fold(mm_nt(left_ed1, w1s))
            to_rows = mm_nt(left_z, s1_ref[i, h])
            yield
            dqs[h] = dq + both_halves(fold(to_rows[: 2 * MB]))
            dks[h] = dk + both_halves(fold(to_rows[2 * MB :]) - dkw)
            dvs[h] = dv
            des[h] = de[:, :1] + jnp.sum(rate_terms, axis=1, keepdims=True)

        return [work(h) for h in range(heads)]

    def store(i, dqs, dks, dvs, des):
        rates, sigs, _ = rates_at(i, qkv_ref[rows_of(i), :])
        dpre = jnp.zeros((MB, LANES), F32)
        for h in range(heads):
            dpre = jnp.where(lax.rem(lane, HEAD) == h, des[h], dpre)
        dqkv_ref[rows_of(i), :] = pack(dqs + dks + dvs + [dpre * rates * (1.0 - sigs)])

    def step(i, now, later, parity):
        outs = [[None] * heads for _ in range(4)]
        behind = jnp.minimum(i + 1, steps - 1)
        interleave(advance(i, now, left[parity]) + finish(behind, left[1 - parity], *outs) + prepare(jnp.maximum(i - 1, 0), later))
        store(behind, *outs)

        @pl.when(resets_ref[block * steps + i] == 1)
        def _():
            gw1[...] += w1[...]
            gb1[...] += b1[...]
            gw2[...] += w2[...]
            gb2[...] += b2[...]

    interleave(prepare(steps - 1, ready[0]))

    def pair(at, carry):
        step(steps - 1 - 2 * at, ready[0], ready[1], 0)
        step(steps - 2 - 2 * at, ready[1], ready[0], 1)
        return carry

    lax.fori_loop(0, steps // 2, pair, 0)
    outs = [[None] * heads for _ in range(4)]
    interleave(finish(0, left[1], *outs))
    store(0, *outs)


def tiles_of(count):
    return -(-count // 2) * LANES


def state_scratch(heads):
    return [
        pltpu.VMEM((heads, HEAD, INNER), F32),
        pltpu.VMEM((heads, MB, INNER), F32),
        pltpu.VMEM((heads, HEAD, INNER), F32),
        pltpu.VMEM((heads, MB, LANES), F32),
    ]


def saved_shapes(total, heads):
    return [
        ((total, heads, LANES, INNER), BF16),
        ((total, heads, LANES, INNER), BF16),
        ((total, heads, MB, INNER), F32),
        ((total, heads, MB, INNER), F32),
        ((total, heads, MB, INNER), F32),
        ((total, heads, MB, LANES), F32),
        ((total, heads, MB, LANES), F32),
        ((total, heads, MB, LANES), F32),
        ((total, heads, MB, LANES), F32),
        ((total, heads, MB, LANES), F32),
    ]


def whole_spec(shape):
    zeros = (0,) * len(shape)
    return pl.BlockSpec(shape, lambda i, *_: zeros)


def own_weights_kernel(heads, owners, all_heads, me_ref, triple_ref, rate_ref, gate_ref, mixer_ref, own_gate_ref):
    for owner in range(owners):
        mine = [head for head in range(owner * heads, (owner + 1) * heads)]

        @pl.when(me_ref[0] == owner)
        def _(mine=mine):
            lane = lane_of((triple_ref.shape[0], LANES))
            none = jnp.zeros(lane.shape, F32)

            def units(ref, group):
                return [pick(ref, group * all_heads + head) if head < all_heads else none for head in mine]

            rate = none
            for at, head in enumerate(mine):
                if head < all_heads:
                    column = jnp.broadcast_to(rate_ref[:, head : head + 1], lane.shape)
                    rate = jnp.where(lax.rem(lane, HEAD) == at, column, rate)
            mixer_ref[...] = pack(units(triple_ref, 0) + units(triple_ref, 1) + units(triple_ref, 2) + [rate])
            own_gate_ref[...] = pack(units(gate_ref, 0))


def own_weights(me, owners, heads, triple, rate, gate, interpret=False):
    block = LANES
    width = triple.shape[0]
    row_spec = lambda columns: pl.BlockSpec((block, columns), lambda i, *_: (i, 0))
    wide = (tiles_of(3 * heads + 1), tiles_of(heads))
    return pl.pallas_call(
        functools.partial(own_weights_kernel, heads, owners, rate.shape[1]),
        grid_spec=pltpu.PrefetchScalarGridSpec(
            num_scalar_prefetch=1,
            grid=(width // block,),
            in_specs=[row_spec(triple.shape[1]), row_spec(rate.shape[1]), row_spec(gate.shape[1])],
            out_specs=[row_spec(columns) for columns in wide],
        ),
        out_shape=[jax.ShapeDtypeStruct((width, columns), F32) for columns in wide],
        compiler_params=pltpu.CompilerParams(dimension_semantics=("arbitrary",), vmem_limit_bytes=32 * 1024 * 1024),
    )(me, triple, rate, gate)


def chain_forward(resets, counts, cols, gate, bias, gain, shift, w1i, b1i, w2i, b2i, steps=8):
    heads = gain.shape[0]
    total = resets.shape[0]
    blocks = total // steps
    token_spec = lambda width: pl.BlockSpec((steps * MB, width), lambda i, *_: (i, 0))
    saved = saved_shapes(total, heads)
    saved_specs = [pl.BlockSpec((steps,) + s[1:], lambda i, *_: (i, 0, 0, 0)) for s, _ in saved]
    params = (bias, gain, shift, w1i, b1i, w2i, b2i)
    wide = tiles_of(heads)
    out = pl.pallas_call(
        functools.partial(fwd_kernel, heads, steps),
        grid_spec=pltpu.PrefetchScalarGridSpec(
            num_scalar_prefetch=2,
            grid=(blocks,),
            in_specs=[token_spec(cols.shape[1]), token_spec(wide)] + [whole_spec(p.shape) for p in params],
            out_specs=[token_spec(wide), token_spec(wide)] + saved_specs,
            scratch_shapes=state_scratch(heads) + 2 * fwd_ready(heads) + 2 * fwd_left(heads),
        ),
        out_shape=[jax.ShapeDtypeStruct((total * MB, wide), F32)] * 2 + [jax.ShapeDtypeStruct(s, d) for s, d in saved],
        compiler_params=pltpu.CompilerParams(dimension_semantics=("arbitrary",), vmem_limit_bytes=56 * 1024 * 1024),
        cost_estimate=pl.CostEstimate(flops=FWD_COST * total, bytes_accessed=1 << 20, transcendentals=0),
    )(resets, counts, cols, gate, *params)
    return out[0], out[1], out[2:]


def chain_backward(resets, counts, cols, bias, cot, gain, shift, saved, part=(0, 8), before=None, steps=8):
    heads = gain.shape[0]
    total = resets.shape[0]
    first = total // steps * part[0] // 8
    blocks = total // steps * part[1] // 8 - first
    last = first + blocks - 1
    token_spec = lambda width: pl.BlockSpec((steps * MB, width), lambda i, *_: (last - i, 0))
    wide = tiles_of(3 * heads + 1)
    saved_specs = [pl.BlockSpec((steps,) + s.shape[1:], lambda i, *_: (last - i, 0, 0, 0)) for s in saved]
    state_shapes = [(heads, HEAD, INNER), (heads, MB, INNER), (heads, HEAD, INNER), (heads, MB, LANES)]
    kept = state_shapes + state_shapes + [(heads, MB, LANES), (heads, MB, LANES)]
    kept_specs = [whole_spec(s) for s in kept]
    before = [] if before is None else list(before)
    out = pl.pallas_call(
        functools.partial(bwd_kernel, heads, steps, first, bool(before)),
        grid_spec=pltpu.PrefetchScalarGridSpec(
            num_scalar_prefetch=2,
            grid=(blocks,),
            in_specs=[token_spec(cols.shape[1]), whole_spec(bias.shape), token_spec(cot.shape[1]), whole_spec(gain.shape), whole_spec(shift.shape)]
            + saved_specs
            + kept_specs[: len(before)],
            out_specs=[pl.BlockSpec((steps * MB, wide), lambda i, *_: (blocks - 1 - i, 0))] + kept_specs,
            scratch_shapes=2 * bwd_ready(heads) + 2 * bwd_left(heads),
        ),
        out_shape=[jax.ShapeDtypeStruct((blocks * steps * MB, wide), F32)] + [jax.ShapeDtypeStruct(s, F32) for s in kept],
        compiler_params=pltpu.CompilerParams(dimension_semantics=("arbitrary",), vmem_limit_bytes=56 * 1024 * 1024),
        cost_estimate=pl.CostEstimate(flops=BWD_COST * blocks * steps, bytes_accessed=1 << 20, transcendentals=0),
    )(resets, counts, cols, bias, cot, gain, shift, *saved, *before)
    return out[0], out[1:]


HEADS = 12
high = lax.Precision.HIGH


def dot(left, right):
    return jnp.dot(left, right, precision=high)


def dot_t(left, right):
    return lax.dot_general(left, right, (((1,), (1,)), ((), ())), precision=high)


def t_dot(left, right):
    return lax.dot_general(left, right, (((0,), (0,)), ((), ())), precision=high)


def swap(value, axis, mask):
    count = lax.axis_size(axis)
    return lax.ppermute(value, axis, [(source, source ^ mask) for source in range(count)])


def bits_of(axis):
    count = lax.axis_size(axis)
    return [1 << at for at in reversed(range(count.bit_length() - 1))]


def upper_of(axis, mask):
    return (lax.axis_index(axis) & mask) != 0


def gather(value, axis, beside=None):
    shape = value.shape
    for done, mask in enumerate(bits_of(axis)):
        other = swap(value, axis, mask)
        if beside is not None and done == 0:
            other, beside = lax.optimization_barrier((other, beside))
        upper = upper_of(axis, mask)
        value = jnp.stack([jnp.where(upper, other, value), jnp.where(upper, value, other)], axis=done)
    value = value.reshape((-1,) + shape)
    return value if beside is None else (value, beside)


def gather_by_distance(value, axis):
    shape = value.shape
    for done, mask in enumerate(bits_of(axis)):
        value = jnp.stack([value, swap(value, axis, mask)], axis=done)
    return value.reshape((-1,) + shape)


def halves(value, axis, mask, dim):
    upper = upper_of(axis, mask)
    lower_half = lax.index_in_dim(value, 0, dim, keepdims=False)
    upper_half = lax.index_in_dim(value, 1, dim, keepdims=False)
    return jnp.where(upper, upper_half, lower_half), jnp.where(upper, lower_half, upper_half)


def row_stages(first=()):
    masks = bits_of("rows")
    order = [mask for mask in first if mask in masks] + [mask for mask in reversed(masks) if mask not in first]
    stages = []
    left = list(masks)
    for mask in order:
        stages.append(("rows", mask, left.index(mask)))
        left.remove(mask)
    return stages


def run_stages(value, stages):
    for axis, mask, dim in stages:
        keep, sent = halves(value, axis, mask, dim)
        value = keep + swap(sent, axis, mask)
    return value


def row_blocks(value):
    count = lax.axis_size("rows")
    return value.reshape((2,) * len(bits_of("rows")) + (value.shape[0] // count,) + value.shape[1:])


def low_bit_blocks(value, other=False):
    n = lax.axis_size("seq")
    share = value.shape[1] // n
    bit = (lax.axis_index("seq") & 1) ^ int(other)
    return jnp.stack([lax.dynamic_slice_in_dim(value, (2 * at + bit) * share, share, 1) for at in range(n // 2)])


def even_first(value):
    n = lax.axis_size("seq")
    share = value.shape[1] // n
    blocks = [value[:, at * share : (at + 1) * share] for at in list(range(0, n, 2)) + list(range(1, n, 2))]
    return jnp.concatenate(blocks, axis=1)


def own_half(value, other=False):
    share = value.shape[1] // 2
    bit = (lax.axis_index("seq") & 1) ^ int(other)
    return lax.dynamic_slice_in_dim(value, bit * share, share, 1)


def columns_to_tokens(value, width):
    n = lax.axis_size("seq")
    tokens = value.shape[0] // n
    moved = lax.all_to_all(value.reshape(n, tokens, -1), "seq", 0, 0)
    return moved.transpose(1, 0, 2).reshape(tokens, -1)[:, :width]


def tokens_to_columns(value):
    n = lax.axis_size("seq")
    tokens = value.shape[0]
    moved = lax.all_to_all(value.reshape(tokens, n, -1).transpose(1, 0, 2), "seq", 0, 0)
    return moved.reshape(n * tokens, -1)


def block_marks(lengths, total):
    block_counts = (lengths + MB - 1) // MB
    begins = (jnp.cumsum(block_counts, dtype=jnp.int32) - block_counts)[None, :]
    index = jnp.arange(total, dtype=jnp.int32)[:, None]
    resets = jnp.any(index == begins, axis=1).astype(jnp.int32)
    inside = jnp.clip(lengths[None, :] - MB * (index - begins), 0, MB)
    return resets, jnp.sum(jnp.where(index >= begins, inside, 0), axis=1)


def own_heads(value, axis, per_head, groups=1):
    n = lax.axis_size("seq")
    me = lax.axis_index("seq")
    count = -(-HEADS // n)
    shape = value.shape
    if n * count == HEADS:
        share = count * per_head
        parts = [lax.dynamic_slice_in_dim(value, g * HEADS * per_head + me * share, share, axis) for g in range(groups)]
        return jnp.concatenate(parts, axis=axis) if groups > 1 else parts[0]
    value = value.reshape(shape[:axis] + (groups, HEADS * per_head) + shape[axis + 1 :])
    pads = [(0, 0)] * value.ndim
    pads[axis + 1] = (0, (n * count - HEADS) * per_head)
    value = jnp.pad(value, pads)
    value = lax.dynamic_slice_in_dim(value, me * count * per_head, count * per_head, axis + 1)
    return value.reshape(shape[:axis] + (groups * count * per_head,) + shape[axis + 1 :])


def pad_columns(value, width):
    return jnp.pad(value, ((0, 0), (0, width - value.shape[1])))


def together(*values):
    return lax.optimization_barrier(values)


def local(
    layer_input,
    doc_lengths,
    output_grad,
    mixer_gain,
    triple_weight,
    rate_weight,
    rate_bias,
    first_weight,
    first_bias,
    second_weight,
    second_bias,
    inner_gain,
    inner_shift,
    gate_weight,
    output_weight,
    feed_gain,
    feed_weight,
    down_weight,
):
    n = lax.axis_size("seq")
    n_rows = lax.axis_size("rows")
    me = lax.axis_index("seq")
    heads = -(-HEADS // n)
    _, tokens, width = layer_input.shape
    span = tokens * n
    ff = down_weight.shape[0]
    head_cols = heads * HEAD
    x = layer_input[0]
    cot = output_grad[0]
    resets, counts = block_marks(doc_lengths[0], span // MB)

    inv = lax.rsqrt(jnp.mean(x * x, axis=-1, keepdims=True) + EPS)
    xhat = x * inv
    normed = xhat * mixer_gain
    split = tiles_of(3 * heads + 1)
    own_mixer, own_gate = own_weights(me[None], n, heads, triple_weight, rate_weight, gate_weight)
    rate_lane = HEAD * (3 * heads % 2)
    bias = jnp.pad(own_heads(rate_bias, 0, 1), (rate_lane, LANES - heads - rate_lane))[None, :]

    def per_head(value, times):
        value = own_heads(value, 0, 1)
        return jnp.concatenate([value] * times, axis=1)[:, None, :]

    gain = per_head(inner_gain, 2)
    shift = per_head(inner_shift, 2)
    w1i = own_heads(first_weight, 0, 1)
    b1i = per_head(first_bias, 1)
    w2t = own_heads(second_weight, 0, 1).transpose(0, 2, 1)
    w2i = w2t - jnp.mean(w2t, axis=1, keepdims=True)
    b2i = per_head(second_bias - jnp.mean(second_bias, axis=1, keepdims=True), 2)
    normed_row, beside = gather(normed, "seq", (own_mixer, own_gate, bias, gain, shift, w1i, b1i, w2i, b2i, resets, counts))
    own_mixer, own_gate, bias, gain, shift, w1i, b1i, w2i, b2i, resets, counts = beside
    normed_row = normed_row.reshape(span, width)
    cols = jnp.dot(normed_row, own_mixer, precision=lax.Precision.HIGHEST)
    gate_pre = dot(normed_row, own_gate)
    gated_cols, mixed, saved = chain_forward(resets, counts, cols, gate_pre, bias, gain, shift, w1i, b1i, w2i, b2i)

    gated = columns_to_tokens(gated_cols[:, :head_cols], width)
    dhidden = dot_t(cot, down_weight)
    gated, dhidden = together(gated, dhidden)
    middle = x + dot(gated, output_weight)
    inv2 = lax.rsqrt(jnp.mean(middle * middle, axis=-1, keepdims=True) + EPS)
    mhat = middle * inv2
    second = mhat * feed_gain
    both = dot(second, feed_weight)
    left, right = both[:, :ff], both[:, ff:]
    sig = jax.nn.sigmoid(left)
    silu = left * sig
    hidden = silu * right
    narrow_stages = row_stages()
    cot_split = even_first(cot)
    down_sum = row_blocks(t_dot(hidden, own_half(cot_split)) + swap(t_dot(hidden, own_half(cot_split, True)), "seq", 1))
    down_keep, down_sent = halves(down_sum, *narrow_stages[0])
    down_other = swap(down_sent, *narrow_stages[0][:2])

    dboth = jnp.concatenate([dhidden * right * (sig + silu * (1.0 - sig)), dhidden * silu], axis=1)
    dsecond = dot_t(dboth, feed_weight)
    feed_gain_part = jnp.sum(dsecond * mhat, axis=0)
    dmhat = dsecond * feed_gain
    dmiddle = cot + inv2 * (dmhat - mhat * jnp.mean(dmhat * mhat, axis=-1, keepdims=True))
    dgated = tokens_to_columns(pad_columns(dot_t(dmiddle, output_weight), n * head_cols))

    second_row = gather_by_distance(second, "seq").reshape(span, width)
    feed_moved = jnp.stack([low_bit_blocks(dboth), swap(low_bit_blocks(dboth, True), "seq", 1)], axis=1)
    dmiddle_split = even_first(dmiddle)
    output_sum = row_blocks(t_dot(gated, own_half(dmiddle_split)) + swap(t_dot(gated, own_half(dmiddle_split, True)), "seq", 1))
    output_keep, output_sent = halves(output_sum, *narrow_stages[0])
    feed_masks = bits_of("seq")[:-1]
    feed_moved = feed_moved.reshape((2,) * len(feed_masks) + (2, tokens, -1))
    for mask in feed_masks[:0:-1]:
        keep, sent = halves(feed_moved, "seq", mask, feed_masks.index(mask))
        feed_moved = jnp.stack([keep, swap(sent, "seq", mask)], axis=feed_masks.index(mask))
        feed_moved = feed_moved.reshape(feed_moved.shape[: feed_masks.index(mask)] + (-1, tokens, feed_moved.shape[-1]))
    feed_keep, feed_sent = halves(feed_moved, "seq", feed_masks[0], 0)
    dgated, output_sent, feed_sent = together(dgated, output_sent, feed_sent)
    feed_other = swap(feed_sent, "seq", feed_masks[0])
    output_other = swap(output_sent, *narrow_stages[0][:2])

    dgated = dgated[:, :head_cols]
    gate_act, gate_slope = gelu_parts(gate_pre[:, :head_cols])[:2]
    dmixed = pad_columns(dgated * gate_act, tiles_of(heads))
    dgate = dgated * mixed[:, :head_cols] * gate_slope
    backward = functools.partial(chain_backward, resets, counts, cols, bias, dmixed, gain, shift, saved)
    part_a, kept = backward(part=(5, 8))

    part_a, kept, down_other, output_other, feed_other, dgate = together(part_a, kept, down_other, output_other, feed_other, dgate)
    dboth_row = jnp.stack([feed_keep, feed_other]).reshape(span, -1)
    feed_cols = dboth_row.shape[1]
    gate_part = t_dot(normed_row, dgate)
    feed = row_blocks(jnp.concatenate([t_dot(second_row, dboth_row), gate_part], axis=1))
    dnormed_gate = dot_t(dgate, own_gate[:, :head_cols])
    feed_stages = row_stages()
    feed_keep, feed_sent = halves(feed, *feed_stages[0])
    narrow = jnp.concatenate([down_keep + down_other, output_keep + output_other], axis=-2)
    narrow_keep, narrow_sent = halves(narrow, *narrow_stages[1])
    kept, feed_sent, narrow_sent, dnormed_gate = together(kept, feed_sent, narrow_sent, dnormed_gate)
    feed_other = swap(feed_sent, *feed_stages[0][:2])
    narrow_other = swap(narrow_sent, *narrow_stages[1][:2])
    part_b, kept = backward(part=(2, 5), before=kept)
    part_b, hidden, middle = together(part_b, hidden, middle)
    layer_output = middle + dot(hidden, down_weight)

    part_b, kept, narrow_other, feed_other = together(part_b, kept, narrow_other, feed_other)
    feed_keep, feed_sent = halves(feed_keep + feed_other, *feed_stages[1])
    narrow_keep, narrow_sent = halves(narrow_keep + narrow_other, *narrow_stages[2])
    kept, feed_sent, narrow_sent = together(kept, feed_sent, narrow_sent)
    feed_other = swap(feed_sent, *feed_stages[1][:2])
    narrow_other = swap(narrow_sent, *narrow_stages[2][:2])
    part_c, kept = backward(part=(0, 2), before=kept)

    part_c, kept, narrow_other, feed_other = together(part_c, kept, narrow_other, feed_other)
    feed = run_stages(feed_keep + feed_other, feed_stages[2:])
    narrow = run_stages(narrow_keep + narrow_other, narrow_stages[3:])
    seq_masks = bits_of("seq")[:-1]
    narrow = jnp.stack(jnp.split(narrow, n // 2, axis=1)).reshape((2,) * len(seq_masks) + (narrow.shape[0], -1))
    narrow = run_stages(narrow, [("seq", mask, seq_masks.index(mask)) for mask in reversed(seq_masks)])
    down_weight_grad, output_weight_grad = narrow[: ff // n_rows], narrow[ff // n_rows :]
    feed_weight_grad, gate_weight_grad = feed[:, :feed_cols], feed[:, feed_cols:]

    dcols = jnp.concatenate([part_c, part_b, part_a])
    triple_part = t_dot(normed_row, dcols)
    triple_blocks = row_blocks(triple_part)
    triple_sum = run_stages(triple_blocks, row_stages())
    dcols, triple_part = together(dcols, triple_part)
    dnormed = dot_t(dcols, own_mixer) + dnormed_gate
    dnormed = dnormed.reshape((2,) * len(bits_of("seq")) + (tokens, width))
    seq_order = [("seq", mask, bits_of("seq").index(mask)) for mask in reversed(bits_of("seq"))]
    dnormed = run_stages(dnormed, seq_order[:-1])
    dnormed_keep, dnormed_sent = halves(dnormed, *seq_order[-1])

    rate_tile = dcols[:, 3 * head_cols - rate_lane :][:, :LANES]
    rate_part = t_dot(rate_tile, normed_row)[rate_lane : rate_lane + heads]
    mixer_gain_part = jnp.sum(triple_part * own_mixer, axis=1)
    mixer_gain_part = (mixer_gain_part + jnp.sum(gate_part * own_gate[:, :head_cols], axis=1)) / mixer_gain
    gw1, gb1, gw2, gb2, ggain, gshift = kept[4:]
    lane_sums = jnp.sum(rate_tile, axis=0)[rate_lane : rate_lane + heads]
    narrow_rows = jnp.concatenate(
        [gb2[:, 0, :HEAD], jnp.sum(ggain, axis=1)[:, :HEAD], jnp.sum(gshift, axis=1)[:, :HEAD], lane_sums[:, None]], axis=1
    )
    pieces = [
        gw1.reshape(-1, INNER),
        gw2.reshape(-1, INNER),
        gb1[:, 0],
        pad_columns(narrow_rows, INNER),
        rate_part.reshape(-1, INNER),
        jnp.stack([mixer_gain_part, feed_gain_part]).reshape(-1, INNER),
    ]
    lengths = [piece.shape[0] for piece in pieces]
    rest = jnp.concatenate(pieces[2:])
    rest = jnp.pad(rest, ((0, -sum(lengths) % (n_rows * 8)), (0, 0)))
    small = jnp.concatenate(pieces[:2] + [rest])
    small, dnormed_sent = together(small, dnormed_sent)
    dnormed_other = swap(dnormed_sent, *seq_order[-1][:2])
    small = run_stages(row_blocks(small), row_stages())
    small = gather(small, "rows")
    small, dnormed_other = together(small, dnormed_other)
    small = gather(small, "seq").reshape(n, -1, INNER)
    starts = [sum(lengths[:at]) for at in range(len(lengths))]
    small = [small[:, start : start + length] for start, length in zip(starts, lengths)]
    first_weight_grad = small[0].reshape(n * heads, HEAD, INNER)[:HEADS]
    second_weight_grad = small[1].reshape(n * heads, HEAD, INNER)[:HEADS].transpose(0, 2, 1)
    first_bias_grad = small[2].reshape(n * heads, INNER)[:HEADS]
    narrow_rows = small[3].reshape(n * heads, INNER)[:HEADS]
    second_bias_grad, inner_gain_grad, inner_shift_grad = (narrow_rows[:, HEAD * at : HEAD * (at + 1)] for at in range(3))
    rate_bias_grad = narrow_rows[:, 3 * HEAD]
    rate_weight_grad = small[4].reshape(n * heads, width)[:HEADS].T
    gains = jnp.sum(small[5], axis=0).reshape(2, width)

    dxhat = (dnormed_keep + dnormed_other) * mixer_gain
    input_grad = dmiddle + inv * (dxhat - xhat * jnp.mean(dxhat * xhat, axis=-1, keepdims=True))

    triple_every = gather(triple_sum, "seq")
    share = 3 * width // n
    if n * heads == HEADS and share % head_cols == 0:
        blocks = []
        for at in range(share // head_cols):
            block = me * (share // head_cols) + at
            columns = lax.dynamic_slice(triple_every, (block % n, 0, block // n * head_cols), (1, triple_every.shape[1], head_cols))
            blocks.append(columns[0])
        triple_weight_grad = jnp.concatenate(blocks, axis=1)
    else:
        every = triple_every[:, :, : 3 * head_cols].reshape(n, -1, 3, head_cols).transpose(1, 2, 0, 3)
        every = every.reshape(every.shape[0], 3, -1)[:, :, :width].reshape(every.shape[0], 3 * width)
        triple_weight_grad = lax.dynamic_slice_in_dim(every, me * share, share, 1)
    if n * heads != HEADS:
        every = gather(gate_weight_grad, "seq").transpose(1, 0, 2)
        every = every.reshape(every.shape[0], -1)[:, :width]
        gate_weight_grad = lax.dynamic_slice_in_dim(every, me * (width // n), width // n, 1)

    return (
        layer_output[None],
        input_grad[None],
        gains[0],
        triple_weight_grad,
        rate_weight_grad,
        rate_bias_grad,
        first_weight_grad,
        first_bias_grad,
        second_weight_grad,
        second_bias_grad,
        inner_gain_grad,
        inner_shift_grad,
        gate_weight_grad,
        output_weight_grad,
        gains[1],
        feed_weight_grad,
        down_weight_grad,
    )


def solution(mesh):
    tokens = P("rows", "seq", None)
    shard = P("rows", "seq")
    in_specs = (tokens, P("rows", None), tokens) + (P(),) * 15
    out_specs = (tokens, tokens, P(), shard) + (P(),) * 8 + (shard, shard, P(), shard, shard)
    return jax.shard_map(local, mesh=mesh, in_specs=in_specs, out_specs=out_specs, check_vma=False)
```

```python
import functools
import jax
import jax.numpy as jnp
from jax import lax
from jax.experimental import pallas as pl
from jax.experimental.pallas import tpu as pltpu
from jax.sharding import PartitionSpec as P

HEAD = 64
INNER = 256
MB = 16
EPS = 1e-06
RTP = 0.7978845608028654
F32 = jnp.float32
BF16 = jnp.bfloat16
LANES = 128
BASE_RATE = 0.1
FWD_COST = 1_500_000_000
BWD_COST = 2_000_000_000


def hi_lo(value):
    high = value.astype(BF16)
    return high, (value - high.astype(F32)).astype(BF16)


def hi_mid_lo(value):
    high = value.astype(BF16)
    rest = value - high.astype(F32)
    mid = rest.astype(BF16)
    return high, mid, (rest - mid.astype(F32)).astype(BF16)


def fold_all(value):
    total = value[:MB]
    for at in range(MB, value.shape[0], MB):
        total = total + value[at : at + MB]
    return total


def six_left(high, mid, low):
    return rows2(high, high, high, mid, mid, low)


def six_right(high, mid, low):
    return rows2(high, mid, low, high, mid, high)


def three_times(value):
    return jnp.concatenate([value, value[:, :HEAD]], axis=1)


def mm(left, right):
    return lax.dot_general(left, right, (((1,), (0,)), ((), ())), preferred_element_type=F32)


def mm_nt(left, right):
    return lax.dot_general(left, right, (((1,), (1,)), ((), ())), preferred_element_type=F32)


def mm_tn(left, right):
    return lax.dot_general(left, right, (((0,), (0,)), ((), ())), preferred_element_type=F32)


def rows2(*parts):
    return jnp.concatenate(parts, axis=0)


def fold(value):
    return value[:MB] + value[MB:]


def half_turn(value):
    return pltpu.roll(value, HEAD, 1)


def both_halves(value):
    return value + half_turn(value)


def lane_of(shape):
    return lax.broadcasted_iota(jnp.int32, shape, 1)


def pick(block, unit):
    tile = block[:, (unit // 2) * LANES : (unit // 2 + 1) * LANES]
    turned = half_turn(tile)
    low_half = lane_of(tile.shape) < HEAD
    if unit % 2 == 0:
        return jnp.where(low_half, tile, turned)
    return jnp.where(low_half, turned, tile)


def pack(parts):
    tiles = []
    for at in range(0, len(parts), 2):
        left = parts[at]
        right = parts[at + 1] if at + 1 < len(parts) else jnp.zeros_like(left)
        tiles.append(jnp.where(lane_of(left.shape) < HEAD, left, right))
    return jnp.concatenate(tiles, axis=1) if len(tiles) > 1 else tiles[0]


def mean_dup(value):
    return jnp.sum(value, axis=1, keepdims=True) * (1.0 / LANES)


def gelu_parts(z):
    z2 = z * z
    t = jnp.tanh(z * (RTP + (RTP * 0.044715) * z2))
    one_t = 0.5 + 0.5 * t
    sech = (1.0 - t) * one_t
    inner = RTP + (RTP * 0.134145) * z2
    act = z * one_t
    zs = z * sech
    slope = one_t + zs * inner
    return act, slope, t, zs, sech, inner


def gelu_curve(z, t, zs, sech, inner):
    return 2.0 * sech * inner + zs * ((2.0 * RTP * 0.134145) * z) - 2.0 * t * zs * inner * inner


def split3(high, low):
    return rows2(high, high, low)


def stack3(high, low):
    return rows2(high, low, high)


def lanes3(value):
    high, low = hi_lo(value)
    lane = lane_of(value.shape)
    return jnp.where((lane >= MB) & (lane < 2 * MB), low.astype(F32), high.astype(F32)).astype(BF16)


def interleave(works):
    works = list(works)
    while works:
        for work in list(works):
            try:
                next(work)
            except StopIteration:
                works.remove(work)


def rates_of(cols, bias_ref, heads, count):
    unit = 3 * heads
    tile = cols[:, (unit // 2) * LANES : (unit // 2 + 1) * LANES] + bias_ref[:1]
    sig = 0.5 + 0.5 * jnp.tanh(0.5 * tile)
    row = lax.broadcasted_iota(jnp.int32, tile.shape, 0)
    return jnp.where(row < count, (BASE_RATE / HEAD) * sig, 0.0), sig, HEAD * (unit % 2)


def put(refs, head, *values):
    for ref, value in zip(refs, values, strict=True):
        ref[head] = value


def take(refs, head):
    return [ref[head] for ref in refs]


def spread_lanes(column, width=LANES):
    return jnp.broadcast_to(column, (MB, width))


def fwd_ready(heads):
    shapes = [((5 * MB, 3 * HEAD), BF16), ((HEAD + 2 * MB, 3 * MB), BF16), ((MB, 3 * MB), F32)] + [((MB, LANES), F32)] * 4
    return [pltpu.VMEM((heads,) + shape, dtype) for shape, dtype in shapes]


def fwd_left(heads):
    shapes = [((2 * MB, INNER), BF16), ((2 * MB, LANES), BF16), ((MB, 3 * MB), F32), ((MB, LANES), F32), ((MB, LANES), F32)]
    return [pltpu.VMEM((heads,) + shape, dtype) for shape, dtype in shapes]


def fwd_kernel(heads, steps, resets_ref, counts_ref, qkv_ref, gate_ref, bias_ref, gain_ref, shift_ref, w1i, b1i, w2i, b2i,
               gated_ref, mixed_ref, s1_ref, s2_ref, z1_ref, zq_ref, m_ref, d2_ref, x_ref, y_ref, r_ref, rq_ref,
               w1, b1, w2, b2, *ready):
    block = pl.program_id(0)
    count = len(fwd_ready(heads))
    ready, left = (ready[:count], ready[count : 2 * count]), ready[2 * count :]
    left = (left[: len(left) // 2], left[len(left) // 2 :])
    lane = lane_of((MB, LANES))
    row = lax.broadcasted_iota(jnp.int32, (MB, LANES), 0)
    lane48 = lane_of((MB, 3 * MB))
    row48 = lax.broadcasted_iota(jnp.int32, (MB, 3 * MB), 0)
    causal = (lane >= HEAD) & (lane < HEAD + MB) & (row <= lane - HEAD)

    def rows_of(i):
        return pl.ds(pl.multiple_of(i * MB, MB), MB)

    def prepare(i, refs):
        qkv = qkv_ref[rows_of(i), :]
        rates, _, rate_lane = rates_of(qkv, bias_ref, heads, counts_ref[block * steps + i])

        def work(h):
            q = pick(qkv, h)
            k = pick(qkv, heads + h)
            v = pick(qkv, 2 * heads + h)
            e = spread_lanes(rates[:, rate_lane + h : rate_lane + h + 1])
            yield
            coef = gain_ref[h] * (shift_ref[h] - v + k)
            khi, klo = hi_lo(k)
            qhi, qlo = hi_lo(q)
            left_a = three_times(rows2(*hi_mid_lo(k), qhi, qlo))
            qsplit = jnp.where(lane < HEAD, qhi.astype(F32), qlo.astype(F32)).astype(BF16)
            zero = jnp.zeros((HEAD, LANES), BF16)
            kq = fold(mm_nt(rows2(khi, klo), rows2(zero, qsplit, zero[: HEAD - MB])))
            yield
            left_d = e * jnp.where(lane < HEAD, k, jnp.where(causal, kq + 1.0, jnp.where((lane >= HEAD + MB) & (lane < HEAD + 2 * MB), 1.0, 0.0)))
            left_d3 = jnp.transpose(stack3(*hi_lo(left_d)))[: HEAD + 2 * MB]
            erow = jnp.transpose(e)[:MB, :]
            e3 = jnp.where(lax.rem(lane48, MB) <= row48, jnp.concatenate([erow, erow, erow], axis=1), 0.0)
            yield
            put(refs, h, left_a, left_d3, e3, e, q, coef, spread_lanes(mean_dup(coef)))

        return [work(h) for h in range(heads)]

    def advance(i, refs, left):
        def work(h):
            left_a, left_d3, e3, e, q, coef, coef_mean = take(refs, h)
            gain = gain_ref[h]
            gain2 = gain * gain
            w1f = w1[h]
            w2f = w2[h]
            w1s = rows2(*hi_mid_lo(w1f))
            w2hi, w2mid, w2lo = hi_mid_lo(w2f)
            w2s = rows2(w2hi, w2mid)
            s1_ref[i, h] = w1s[: 2 * HEAD]
            s2_ref[i, h] = w2s
            b1v = b1[h]
            b2v = b2[h]
            z = mm(left_a, w1s)
            yield
            z1 = fold_all(z[: 3 * MB]) + b1v
            act, slope = gelu_parts(z1)[:2]
            ahi, alo, arest = hi_mid_lo(act)
            z2 = fold_all(mm_nt(rows2(ahi, alo, arest), rows2(w2s, w2lo, jnp.zeros((HEAD, INNER), BF16))))
            yield
            z2 = both_halves(z2[:, :LANES] + z2[:, LANES:]) + b2v
            yield
            g2z = gain2 * z2
            inv = lax.rsqrt(mean_dup(z2 * z2) + EPS)
            m1 = mean_dup(g2z)
            m2 = mean_dup(g2z * z2)
            m3 = mean_dup(coef * z2)
            yield
            x = z2 * inv
            g = gain2 * x + coef
            d2 = inv * (g - (inv * m1 + coef_mean) - x * (inv * inv * m2 + inv * m3))
            d2hi, d2lo = hi_lo(d2)
            m = fold(mm(rows2(d2hi, d2lo), w2s))
            yield
            d1 = m * slope
            u = mm(left_d3, split3(*hi_lo(d1)))
            yield
            w1[h] = w1f - u[:HEAD]
            b1[h] = b1v - u[HEAD + MB :]
            ed2 = e * d2
            w2[h] = w2f - mm(jnp.transpose(six_left(*hi_mid_lo(ed2)))[:HEAD], six_right(ahi, alo, arest))
            b2[h] = b2v - jnp.sum(ed2, axis=0, keepdims=True)
            z1_ref[i, h] = z1
            zq_ref[i, h] = fold(z[3 * MB :]) + b1v - u[HEAD : HEAD + MB]
            m_ref[i, h] = m
            d2_ref[i, h] = d2
            x_ref[i, h] = x
            r_ref[i, h] = spread_lanes(inv)
            put(left, h, rows2(ahi, alo), rows2(d2hi, d2lo), e3, q, b2v)

        return [work(h) for h in range(heads)]

    def finish(i, left, outs):
        def work(h):
            left_b, left_c, e3, q, b2v = take(left, h)
            ahi, alo = left_b[:MB], left_b[MB:]
            w2s = s2_ref[i, h]
            qact = gelu_parts(zq_ref[i, h])[0]
            qahi, qalo = hi_lo(qact)
            left_e = rows2(qahi, qalo)
            uq = fold(mm_nt(left_e, rows2(ahi, ahi, ahi))) + mm_nt(qahi, rows2(alo, alo, alo))
            z2q = fold(mm_nt(left_e, w2s))
            yield
            r3 = lanes3(e3 * (uq + 1.0))
            z2q = both_halves(z2q) + b2v - mm(r3, split3(left_c[:MB], left_c[MB:]))
            yield
            invq = lax.rsqrt(mean_dup(z2q * z2q) + EPS)
            yield
            y = z2q * invq
            outs[h] = q + gain_ref[h] * y + shift_ref[h]
            y_ref[i, h] = y
            rq_ref[i, h] = spread_lanes(invq)

        return [work(h) for h in range(heads)]

    def store(i, outs):
        mixed = pack(outs)
        mixed_ref[rows_of(i), :] = mixed
        gated_ref[rows_of(i), :] = gelu_parts(gate_ref[rows_of(i), :])[0] * mixed

    def step(i, now, later, parity):
        @pl.when(resets_ref[block * steps + i] == 1)
        def _():
            w1[...] = w1i[...]
            b1[...] = jnp.broadcast_to(b1i[...], b1.shape)
            w2[...] = w2i[...]
            b2[...] = jnp.broadcast_to(b2i[...], b2.shape)

        outs = [None] * heads
        behind = jnp.maximum(i - 1, 0)
        interleave(advance(i, now, left[parity]) + finish(behind, left[1 - parity], outs) + prepare(jnp.minimum(i + 1, steps - 1), later))
        store(behind, outs)

    interleave(prepare(0, ready[0]))

    def pair(at, carry):
        step(2 * at, ready[0], ready[1], 0)
        step(2 * at + 1, ready[1], ready[0], 1)
        return carry

    lax.fori_loop(0, steps // 2, pair, 0)
    outs = [None] * heads
    interleave(finish(steps - 1, left[1], outs))
    store(steps - 1, outs)


def bwd_ready(heads):
    halves = [(2 * MB, LANES), (HEAD + MB, 6 * MB), (2 * MB, INNER), (2 * MB, INNER), (2 * MB, INNER), (2 * MB, INNER), (2 * MB, LANES), (HEAD, 6 * MB)]
    wide = [(MB, INNER)] * 4
    rest = [(MB, LANES)] * 11
    shapes = [(shape, BF16) for shape in halves] + [(shape, F32) for shape in wide + rest]
    return [pltpu.VMEM((heads,) + shape, dtype) for shape, dtype in shapes]


def bwd_left(heads):
    shapes = [((LANES, INNER), BF16), ((4 * MB, INNER), BF16), ((2 * MB, INNER), BF16)] + [((MB, LANES), F32)] * 5
    return [pltpu.VMEM((heads,) + shape, dtype) for shape, dtype in shapes]


def bwd_kernel(heads, steps, first_block, begun, resets_ref, counts_ref, qkv_ref, bias_ref, cot_ref, gain_ref, shift_ref,
               s1_ref, s2_ref, z1_ref, zq_ref, m_ref, d2_ref, x_ref, y_ref, r_ref, rq_ref, *refs):
    before = refs[:10] if begun else None
    dqkv_ref, w1, b1, w2, b2, gw1, gb1, gw2, gb2, ggain, gshift, *ready = refs[10 if begun else 0 :]
    count = len(bwd_ready(heads))
    ready, left = (ready[:count], ready[count : 2 * count]), ready[2 * count :]
    left = (left[: len(left) // 2], left[len(left) // 2 :])
    blocks = pl.num_programs(0)
    block = first_block + blocks - 1 - pl.program_id(0)
    lane = lane_of((MB, LANES))
    lane48 = lane_of((MB, 3 * MB))
    row48 = lax.broadcasted_iota(jnp.int32, (MB, 3 * MB), 0)
    causal3 = row48 <= lax.rem(lane48, MB)
    counted = causal3 & (lane48 < MB)

    @pl.when(pl.program_id(0) == 0)
    def _():
        for at, ref in enumerate((w1, b1, w2, b2, gw1, gb1, gw2, gb2, ggain, gshift)):
            ref[...] = before[at][...] if begun else jnp.zeros_like(ref)

    def rows_of(i):
        return pl.ds(pl.multiple_of(i * MB, MB), MB)

    def rates_at(i, qkv):
        return rates_of(qkv, bias_ref, heads, counts_ref[block * steps + i])

    def prepare(i, refs):
        qkv = qkv_ref[rows_of(i), :]
        rates, sigs, rate_lane = rates_at(i, qkv)
        cots = cot_ref[rows_of(i), :]

        def work(h):
            gain = gain_ref[h]
            gain2 = gain * gain
            q = pick(qkv, h)
            k = pick(qkv, heads + h)
            v = pick(qkv, 2 * heads + h)
            cot = pick(cots, h)
            ecol = rates[:, rate_lane + h : rate_lane + h + 1]
            e = spread_lanes(ecol)
            e256 = spread_lanes(ecol, INNER)
            e3 = jnp.where(causal3, spread_lanes(ecol, 3 * MB), 0.0)
            khi, klo = hi_lo(k)
            qhi, qlo = hi_lo(q)
            left_k = rows2(khi, klo)
            qsplit = jnp.where(lane < HEAD, qhi.astype(F32), qlo.astype(F32)).astype(BF16)
            kq3 = fold(mm_nt(left_k, rows2(qsplit, qsplit, qsplit))) + 1.0
            yield
            pt3 = lanes3(e3 * kq3)
            ones = jnp.where(lane < HEAD + MB, 1.0, 0.0)
            qone = hi_lo(jnp.where(lane < HEAD, q, ones))
            kone = hi_lo(jnp.where(lane < HEAD, k, ones))
            left_q = jnp.transpose(rows2(stack3(*qone), stack3(*kone)))[: HEAD + MB]
            z1 = z1_ref[i, h]
            zq = zq_ref[i, h]
            m = m_ref[i, h]
            d2 = d2_ref[i, h]
            x = x_ref[i, h]
            y = y_ref[i, h]
            invq = rq_ref[i, h]
            act, slope, t, zs, sech, inner = gelu_parts(z1)
            curve = gelu_curve(z1, t, zs, sech, inner)
            qact, qslope = gelu_parts(zq)[:2]
            ahi, alo = hi_lo(act)
            qahi, qalo = hi_lo(qact)
            d1 = m * slope
            d1hi, d1lo = hi_lo(d1)
            d2hi, d2lo = hi_lo(d2)
            dy = gain * cot
            dy_mean = mean_dup(dy)
            dyy_mean = mean_dup(dy * y)
            yield
            dz2q = invq * (dy - dy_mean - y * dyy_mean)
            zhi, zlo = hi_lo(dz2q)
            dqa = fold(mm(rows2(zhi, zlo), s2_ref[i, h]))
            yield
            left_a = rows2(ahi, alo)
            aq3 = fold(mm_nt(left_a, rows2(qahi, qahi, qahi))) + mm_nt(ahi, rows2(qalo, qalo, qalo)) + 1.0
            yield
            zsplit = jnp.where(lane < HEAD, zhi.astype(F32), zlo.astype(F32)).astype(BF16)
            drt3 = -fold(mm_nt(rows2(d2hi, d2lo), rows2(zsplit, zsplit, zsplit)))
            yield
            rt3 = lanes3(e3 * aq3)
            dd2 = -mm(rt3, split3(zhi, zlo))
            de = jnp.sum(jnp.where(counted, drt3 * aq3, 0.0), axis=1, keepdims=True)
            du2t = e3 * drt3
            du2t_hi, du2t_lo = hi_lo(du2t[:, :MB])
            dqa = dqa + mm_tn(rows2(du2t_hi, du2t_lo, du2t_hi), split3(ahi, alo))
            yield
            da = mm(lanes3(du2t), split3(qahi, qalo))
            dzq = dqa * qslope
            zqhi, zqlo = hi_lo(dzq)
            dpt3 = -(fold(mm_nt(rows2(d1hi, d1lo), rows2(zqhi, zqhi, zqhi))) + mm_nt(d1hi, rows2(zqlo, zqlo, zqlo)))
            yield
            dd1 = -mm(pt3, split3(zqhi, zqlo))
            de = de + jnp.sum(jnp.where(counted, dpt3 * kq3, 0.0), axis=1, keepdims=True)
            du1t = e3 * dpt3
            du1t_hi, du1t_lo = hi_lo(du1t[:, :MB])
            dq = cot + mm_tn(rows2(du1t_hi, du1t_lo, du1t_hi), split3(khi, klo))
            dk = mm(lanes3(du1t), split3(qhi, qlo))
            yield
            left_2 = jnp.transpose(rows2(stack3(zhi, zlo), stack3(d2hi, d2lo)))[:HEAD]
            target = shift_ref[h] - v + k
            g = gain2 * x + gain * target
            put(
                refs, h, left_k, left_q, left_a, rows2(qahi, qalo), rows2(zqhi, zqlo), rows2(*hi_lo(e256 * d1)), rows2(*hi_lo(e * d2)), left_2,
                slope, m * curve, dd1, da,
                dd2, dq, dk, spread_lanes(de), dz2q, cot * y, cot, g, spread_lanes(mean_dup(g * x)), 2.0 * gain * x + target, e,
            )

        return [work(h) for h in range(heads)]

    def advance(i, refs, left):
        following = resets_ref[jnp.minimum(block * steps + i + 1, resets_ref.shape[0] - 1)]
        carry_on = jnp.where(following == 1, 0.0, 1.0)

        def work(h):
            left_k, left_q, left_a, left_qa, left_zq, left_ed1, left_ed2, left_2, slope, mcurve, dd1, da, *rest = take(refs, h)
            dd2, dq, dk, de, dz2q, gain_part, cot, g, mgx, gain_factor, e = rest
            gain = gain_ref[h]
            gain2 = gain * gain
            s2 = s2_ref[i, h]
            m = m_ref[i, h]
            d2 = d2_ref[i, h]
            x = x_ref[i, h]
            inv = r_ref[i, h]
            w1f = w1[h] * carry_on
            w2f = w2[h] * carry_on
            b1v = b1[h] * carry_on
            b2v = b2[h] * carry_on
            w1s = rows2(*hi_lo(w1f))
            w2s = rows2(*hi_lo(w2f))
            de1 = -(fold(mm(left_k, w1s)) + b1v)
            yield
            e256 = jnp.concatenate([e, e], axis=1)
            dd1 = dd1 + e256 * de1
            dm = dd1 * slope
            dmhi, dmlo = hi_lo(dm)
            de2 = -(both_halves(fold(mm_nt(left_a, w2s))) + b2v)
            back = both_halves(fold(mm_nt(rows2(dmhi, dmlo), s2)))
            yield
            dd2 = dd2 + e * de2 + back
            yield
            q1 = mean_dup(dd2)
            q2 = mean_dup(dd2 * x)
            dr_r = mean_dup(dd2 * d2)
            yield
            dg = inv * (dd2 - q1 - x * q2)
            dx = dg * gain2 - inv * (dd2 * mgx + g * q2)
            x1 = mean_dup(dx)
            x2 = mean_dup(dx * x)
            yield
            dz2 = inv * (dx - x1 - x * x2) - x * inv * dr_r
            dz2hi, dz2lo = hi_lo(dz2)
            da = da - fold(mm(left_ed2, w2s)) + fold(mm(rows2(dz2hi, dz2lo), s2))
            yield
            dz1 = dd1 * mcurve + da * slope
            z1hi, z1lo = hi_lo(dz1)
            zqhi, zqlo = left_zq[:MB], left_zq[MB:]
            grads = mm(left_q, rows2(split3(zqhi, zqlo), split3(z1hi, z1lo)))
            yield
            w1[h] = w1f + grads[:HEAD]
            b1[h] = b1v + grads[HEAD:]
            ahi, alo = left_a[:MB], left_a[MB:]
            qahi, qalo = left_qa[:MB], left_qa[MB:]
            left_3 = jnp.transpose(stack3(dz2hi, dz2lo))[:HEAD]
            w2[h] = w2f + mm(left_2, rows2(split3(qahi, qalo), split3(dmhi, dmlo))) + mm(left_3, split3(ahi, alo))
            b2[h] = b2v + jnp.sum(dz2q + dz2, axis=0, keepdims=True)
            dgg = dg * gain
            rate_terms = m * slope * de1
            rate_terms = rate_terms[:, :LANES] + rate_terms[:, LANES:] + 0.5 * (d2 * de2)
            ggain[h] += gain_part + dg * gain_factor
            gshift[h] += cot + dgg
            put(left, h, w1s, rows2(left_zq, z1hi, z1lo), left_ed1, dq, dk + dgg, -dgg, de, rate_terms)

        return [work(h) for h in range(heads)]

    def finish(i, left, dqs, dks, dvs, des):
        def work(h):
            w1s, left_z, left_ed1, dq, dk, dv, de, rate_terms = take(left, h)
            dkw = fold(mm_nt(left_ed1, w1s))
            to_rows = mm_nt(left_z, s1_ref[i, h])
            yield
            dqs[h] = dq + both_halves(fold(to_rows[: 2 * MB]))
            dks[h] = dk + both_halves(fold(to_rows[2 * MB :]) - dkw)
            dvs[h] = dv
            des[h] = de[:, :1] + jnp.sum(rate_terms, axis=1, keepdims=True)

        return [work(h) for h in range(heads)]

    def store(i, dqs, dks, dvs, des):
        rates, sigs, _ = rates_at(i, qkv_ref[rows_of(i), :])
        dpre = jnp.zeros((MB, LANES), F32)
        for h in range(heads):
            dpre = jnp.where(lax.rem(lane, HEAD) == h, des[h], dpre)
        dqkv_ref[rows_of(i), :] = pack(dqs + dks + dvs + [dpre * rates * (1.0 - sigs)])

    def step(i, now, later, parity):
        outs = [[None] * heads for _ in range(4)]
        behind = jnp.minimum(i + 1, steps - 1)
        interleave(advance(i, now, left[parity]) + finish(behind, left[1 - parity], *outs) + prepare(jnp.maximum(i - 1, 0), later))
        store(behind, *outs)

        @pl.when(resets_ref[block * steps + i] == 1)
        def _():
            gw1[...] += w1[...]
            gb1[...] += b1[...]
            gw2[...] += w2[...]
            gb2[...] += b2[...]

    interleave(prepare(steps - 1, ready[0]))

    def pair(at, carry):
        step(steps - 1 - 2 * at, ready[0], ready[1], 0)
        step(steps - 2 - 2 * at, ready[1], ready[0], 1)
        return carry

    lax.fori_loop(0, steps // 2, pair, 0)
    outs = [[None] * heads for _ in range(4)]
    interleave(finish(0, left[1], *outs))
    store(0, *outs)


def tiles_of(count):
    return -(-count // 2) * LANES


def state_scratch(heads):
    return [
        pltpu.VMEM((heads, HEAD, INNER), F32),
        pltpu.VMEM((heads, MB, INNER), F32),
        pltpu.VMEM((heads, HEAD, INNER), F32),
        pltpu.VMEM((heads, MB, LANES), F32),
    ]


def saved_shapes(total, heads):
    return [
        ((total, heads, LANES, INNER), BF16),
        ((total, heads, LANES, INNER), BF16),
        ((total, heads, MB, INNER), F32),
        ((total, heads, MB, INNER), F32),
        ((total, heads, MB, INNER), F32),
        ((total, heads, MB, LANES), F32),
        ((total, heads, MB, LANES), F32),
        ((total, heads, MB, LANES), F32),
        ((total, heads, MB, LANES), F32),
        ((total, heads, MB, LANES), F32),
    ]


def whole_spec(shape):
    zeros = (0,) * len(shape)
    return pl.BlockSpec(shape, lambda i, *_: zeros)


def own_weights_kernel(heads, owners, all_heads, me_ref, triple_ref, rate_ref, gate_ref, mixer_ref, own_gate_ref):
    for owner in range(owners):
        mine = [head for head in range(owner * heads, (owner + 1) * heads)]

        @pl.when(me_ref[0] == owner)
        def _(mine=mine):
            lane = lane_of((triple_ref.shape[0], LANES))
            none = jnp.zeros(lane.shape, F32)

            def units(ref, group):
                return [pick(ref, group * all_heads + head) if head < all_heads else none for head in mine]

            rate = none
            for at, head in enumerate(mine):
                if head < all_heads:
                    column = jnp.broadcast_to(rate_ref[:, head : head + 1], lane.shape)
                    rate = jnp.where(lax.rem(lane, HEAD) == at, column, rate)
            mixer_ref[...] = pack(units(triple_ref, 0) + units(triple_ref, 1) + units(triple_ref, 2) + [rate])
            own_gate_ref[...] = pack(units(gate_ref, 0))


def own_weights(me, owners, heads, triple, rate, gate):
    block = LANES
    width = triple.shape[0]
    row_spec = lambda columns: pl.BlockSpec((block, columns), lambda i, *_: (i, 0))
    wide = (tiles_of(3 * heads + 1), tiles_of(heads))
    return pl.pallas_call(
        functools.partial(own_weights_kernel, heads, owners, rate.shape[1]),
        grid_spec=pltpu.PrefetchScalarGridSpec(
            num_scalar_prefetch=1,
            grid=(width // block,),
            in_specs=[row_spec(triple.shape[1]), row_spec(rate.shape[1]), row_spec(gate.shape[1])],
            out_specs=[row_spec(columns) for columns in wide],
        ),
        out_shape=[jax.ShapeDtypeStruct((width, columns), F32) for columns in wide],
        compiler_params=pltpu.CompilerParams(dimension_semantics=("arbitrary",), vmem_limit_bytes=32 * 1024 * 1024),
    )(me, triple, rate, gate)


def chain_forward(resets, counts, cols, gate, bias, gain, shift, w1i, b1i, w2i, b2i, steps=16):
    heads = gain.shape[0]
    total = resets.shape[0]
    blocks = total // steps
    token_spec = lambda width: pl.BlockSpec((steps * MB, width), lambda i, *_: (i, 0))
    saved = saved_shapes(total, heads)
    saved_specs = [pl.BlockSpec((steps,) + s[1:], lambda i, *_: (i, 0, 0, 0)) for s, _ in saved]
    params = (bias, gain, shift, w1i, b1i, w2i, b2i)
    wide = tiles_of(heads)
    out = pl.pallas_call(
        functools.partial(fwd_kernel, heads, steps),
        grid_spec=pltpu.PrefetchScalarGridSpec(
            num_scalar_prefetch=2,
            grid=(blocks,),
            in_specs=[token_spec(cols.shape[1]), token_spec(wide)] + [whole_spec(p.shape) for p in params],
            out_specs=[token_spec(wide), token_spec(wide)] + saved_specs,
            scratch_shapes=state_scratch(heads) + 2 * fwd_ready(heads) + 2 * fwd_left(heads),
        ),
        out_shape=[jax.ShapeDtypeStruct((total * MB, wide), F32)] * 2 + [jax.ShapeDtypeStruct(s, d) for s, d in saved],
        compiler_params=pltpu.CompilerParams(dimension_semantics=("arbitrary",), vmem_limit_bytes=56 * 1024 * 1024),
        cost_estimate=pl.CostEstimate(flops=FWD_COST * total, bytes_accessed=1 << 20, transcendentals=0),
    )(resets, counts, cols, gate, *params)
    return out[0], out[1], out[2:]


def chain_backward(resets, counts, cols, bias, cot, gain, shift, saved, part=(0, 8), before=None, steps=8):
    heads = gain.shape[0]
    total = resets.shape[0]
    first = total // steps * part[0] // 8
    blocks = total // steps * part[1] // 8 - first
    last = first + blocks - 1
    token_spec = lambda width: pl.BlockSpec((steps * MB, width), lambda i, *_: (last - i, 0))
    wide = tiles_of(3 * heads + 1)
    saved_specs = [pl.BlockSpec((steps,) + s.shape[1:], lambda i, *_: (last - i, 0, 0, 0)) for s in saved]
    state_shapes = [(heads, HEAD, INNER), (heads, MB, INNER), (heads, HEAD, INNER), (heads, MB, LANES)]
    kept = state_shapes + state_shapes + [(heads, MB, LANES), (heads, MB, LANES)]
    kept_specs = [whole_spec(s) for s in kept]
    before = [] if before is None else list(before)
    out = pl.pallas_call(
        functools.partial(bwd_kernel, heads, steps, first, bool(before)),
        grid_spec=pltpu.PrefetchScalarGridSpec(
            num_scalar_prefetch=2,
            grid=(blocks,),
            in_specs=[token_spec(cols.shape[1]), whole_spec(bias.shape), token_spec(cot.shape[1]), whole_spec(gain.shape), whole_spec(shift.shape)]
            + saved_specs
            + kept_specs[: len(before)],
            out_specs=[pl.BlockSpec((steps * MB, wide), lambda i, *_: (blocks - 1 - i, 0))] + kept_specs,
            scratch_shapes=2 * bwd_ready(heads) + 2 * bwd_left(heads),
        ),
        out_shape=[jax.ShapeDtypeStruct((blocks * steps * MB, wide), F32)] + [jax.ShapeDtypeStruct(s, F32) for s in kept],
        compiler_params=pltpu.CompilerParams(dimension_semantics=("arbitrary",), vmem_limit_bytes=56 * 1024 * 1024),
        cost_estimate=pl.CostEstimate(flops=BWD_COST * blocks * steps, bytes_accessed=1 << 20, transcendentals=0),
    )(resets, counts, cols, bias, cot, gain, shift, *saved, *before)
    return out[0], out[1:]


HEADS = 12
high = lax.Precision.HIGH


def dot(left, right):
    return jnp.dot(left, right, precision=high)


def dot_t(left, right):
    return lax.dot_general(left, right, (((1,), (1,)), ((), ())), precision=high)


def t_dot(left, right):
    return lax.dot_general(left, right, (((0,), (0,)), ((), ())), precision=high)


def swap(value, axis, mask):
    count = lax.axis_size(axis)
    return lax.ppermute(value, axis, [(source, source ^ mask) for source in range(count)])


def bits_of(axis):
    count = lax.axis_size(axis)
    return [1 << at for at in reversed(range(count.bit_length() - 1))]


def upper_of(axis, mask):
    return (lax.axis_index(axis) & mask) != 0


def gather(value, axis, beside=None):
    shape = value.shape
    for done, mask in enumerate(bits_of(axis)):
        other = swap(value, axis, mask)
        if beside is not None and done == 0:
            other, beside = lax.optimization_barrier((other, beside))
        upper = upper_of(axis, mask)
        value = jnp.stack([jnp.where(upper, other, value), jnp.where(upper, value, other)], axis=done)
    value = value.reshape((-1,) + shape)
    return value if beside is None else (value, beside)


def gather_by_distance(value, axis):
    shape = value.shape
    for done, mask in enumerate(bits_of(axis)):
        value = jnp.stack([value, swap(value, axis, mask)], axis=done)
    return value.reshape((-1,) + shape)


def halves(value, axis, mask, dim):
    upper = upper_of(axis, mask)
    lower_half = lax.index_in_dim(value, 0, dim, keepdims=False)
    upper_half = lax.index_in_dim(value, 1, dim, keepdims=False)
    return jnp.where(upper, upper_half, lower_half), jnp.where(upper, lower_half, upper_half)


def row_stages(first=()):
    masks = bits_of("rows")
    order = [mask for mask in first if mask in masks] + [mask for mask in reversed(masks) if mask not in first]
    stages = []
    left = list(masks)
    for mask in order:
        stages.append(("rows", mask, left.index(mask)))
        left.remove(mask)
    return stages


def run_stages(value, stages):
    for axis, mask, dim in stages:
        keep, sent = halves(value, axis, mask, dim)
        value = keep + swap(sent, axis, mask)
    return value


def row_blocks(value):
    count = lax.axis_size("rows")
    return value.reshape((2,) * len(bits_of("rows")) + (value.shape[0] // count,) + value.shape[1:])


def low_bit_blocks(value, other=False):
    n = lax.axis_size("seq")
    share = value.shape[1] // n
    bit = (lax.axis_index("seq") & 1) ^ int(other)
    return jnp.stack([lax.dynamic_slice_in_dim(value, (2 * at + bit) * share, share, 1) for at in range(n // 2)])


def even_first(value):
    n = lax.axis_size("seq")
    share = value.shape[1] // n
    blocks = [value[:, at * share : (at + 1) * share] for at in list(range(0, n, 2)) + list(range(1, n, 2))]
    return jnp.concatenate(blocks, axis=1)


def own_half(value, other=False):
    share = value.shape[1] // 2
    bit = (lax.axis_index("seq") & 1) ^ int(other)
    return lax.dynamic_slice_in_dim(value, bit * share, share, 1)


def columns_to_tokens(value, width):
    n = lax.axis_size("seq")
    tokens = value.shape[0] // n
    moved = lax.all_to_all(value.reshape(n, tokens, -1), "seq", 0, 0)
    return moved.transpose(1, 0, 2).reshape(tokens, -1)[:, :width]


def tokens_to_columns(value):
    n = lax.axis_size("seq")
    tokens = value.shape[0]
    moved = lax.all_to_all(value.reshape(tokens, n, -1).transpose(1, 0, 2), "seq", 0, 0)
    return moved.reshape(n * tokens, -1)


def block_marks(lengths, total):
    block_counts = (lengths + MB - 1) // MB
    begins = (jnp.cumsum(block_counts, dtype=jnp.int32) - block_counts)[None, :]
    index = jnp.arange(total, dtype=jnp.int32)[:, None]
    resets = jnp.any(index == begins, axis=1).astype(jnp.int32)
    inside = jnp.clip(lengths[None, :] - MB * (index - begins), 0, MB)
    return resets, jnp.sum(jnp.where(index >= begins, inside, 0), axis=1)


def own_heads(value, axis, per_head, groups=1):
    n = lax.axis_size("seq")
    me = lax.axis_index("seq")
    count = -(-HEADS // n)
    shape = value.shape
    if n * count == HEADS:
        share = count * per_head
        parts = [lax.dynamic_slice_in_dim(value, g * HEADS * per_head + me * share, share, axis) for g in range(groups)]
        return jnp.concatenate(parts, axis=axis) if groups > 1 else parts[0]
    value = value.reshape(shape[:axis] + (groups, HEADS * per_head) + shape[axis + 1 :])
    pads = [(0, 0)] * value.ndim
    pads[axis + 1] = (0, (n * count - HEADS) * per_head)
    value = jnp.pad(value, pads)
    value = lax.dynamic_slice_in_dim(value, me * count * per_head, count * per_head, axis + 1)
    return value.reshape(shape[:axis] + (groups * count * per_head,) + shape[axis + 1 :])


def pad_columns(value, width):
    return jnp.pad(value, ((0, 0), (0, width - value.shape[1])))


def together(*values):
    return lax.optimization_barrier(values)


def local(
    layer_input,
    doc_lengths,
    output_grad,
    mixer_gain,
    triple_weight,
    rate_weight,
    rate_bias,
    first_weight,
    first_bias,
    second_weight,
    second_bias,
    inner_gain,
    inner_shift,
    gate_weight,
    output_weight,
    feed_gain,
    feed_weight,
    down_weight,
):
    n = lax.axis_size("seq")
    n_rows = lax.axis_size("rows")
    me = lax.axis_index("seq")
    heads = -(-HEADS // n)
    _, tokens, width = layer_input.shape
    span = tokens * n
    ff = down_weight.shape[0]
    head_cols = heads * HEAD
    x = layer_input[0]
    cot = output_grad[0]
    resets, counts = block_marks(doc_lengths[0], span // MB)

    inv = lax.rsqrt(jnp.mean(x * x, axis=-1, keepdims=True) + EPS)
    xhat = x * inv
    normed = xhat * mixer_gain
    split = tiles_of(3 * heads + 1)
    own_mixer, own_gate = own_weights(me[None], n, heads, triple_weight, rate_weight, gate_weight)
    rate_lane = HEAD * (3 * heads % 2)
    bias = jnp.pad(own_heads(rate_bias, 0, 1), (rate_lane, LANES - heads - rate_lane))[None, :]

    def per_head(value, times):
        value = own_heads(value, 0, 1)
        return jnp.concatenate([value] * times, axis=1)[:, None, :]

    gain = per_head(inner_gain, 2)
    shift = per_head(inner_shift, 2)
    w1i = own_heads(first_weight, 0, 1)
    b1i = per_head(first_bias, 1)
    w2t = own_heads(second_weight, 0, 1).transpose(0, 2, 1)
    w2i = w2t - jnp.mean(w2t, axis=1, keepdims=True)
    b2i = per_head(second_bias - jnp.mean(second_bias, axis=1, keepdims=True), 2)
    normed_row, beside = gather(normed, "seq", (own_mixer, own_gate, bias, gain, shift, w1i, b1i, w2i, b2i, resets, counts))
    own_mixer, own_gate, bias, gain, shift, w1i, b1i, w2i, b2i, resets, counts = beside
    normed_row = normed_row.reshape(span, width)
    cols = jnp.dot(normed_row, own_mixer, precision=lax.Precision.HIGHEST)
    gate_pre = dot(normed_row, own_gate)
    gated_cols, mixed, saved = chain_forward(resets, counts, cols, gate_pre, bias, gain, shift, w1i, b1i, w2i, b2i)

    gated = columns_to_tokens(gated_cols[:, :head_cols], width)
    dhidden = dot_t(cot, down_weight)
    gated, dhidden = together(gated, dhidden)
    middle = x + dot(gated, output_weight)
    inv2 = lax.rsqrt(jnp.mean(middle * middle, axis=-1, keepdims=True) + EPS)
    mhat = middle * inv2
    second = mhat * feed_gain
    both = dot(second, feed_weight)
    left, right = both[:, :ff], both[:, ff:]
    sig = jax.nn.sigmoid(left)
    silu = left * sig
    hidden = silu * right
    narrow_stages = row_stages()
    cot_split = even_first(cot)
    down_sum = row_blocks(t_dot(hidden, own_half(cot_split)) + swap(t_dot(hidden, own_half(cot_split, True)), "seq", 1))
    down_keep, down_sent = halves(down_sum, *narrow_stages[0])
    down_other = swap(down_sent, *narrow_stages[0][:2])

    dboth = jnp.concatenate([dhidden * right * (sig + silu * (1.0 - sig)), dhidden * silu], axis=1)
    dsecond = dot_t(dboth, feed_weight)
    feed_gain_part = jnp.sum(dsecond * mhat, axis=0)
    dmhat = dsecond * feed_gain
    dmiddle = cot + inv2 * (dmhat - mhat * jnp.mean(dmhat * mhat, axis=-1, keepdims=True))
    dgated = tokens_to_columns(pad_columns(dot_t(dmiddle, output_weight), n * head_cols))

    second_row = gather_by_distance(second, "seq").reshape(span, width)
    feed_moved = jnp.stack([low_bit_blocks(dboth), swap(low_bit_blocks(dboth, True), "seq", 1)], axis=1)
    dmiddle_split = even_first(dmiddle)
    output_sum = row_blocks(t_dot(gated, own_half(dmiddle_split)) + swap(t_dot(gated, own_half(dmiddle_split, True)), "seq", 1))
    output_keep, output_sent = halves(output_sum, *narrow_stages[0])
    feed_masks = bits_of("seq")[:-1]
    feed_moved = feed_moved.reshape((2,) * len(feed_masks) + (2, tokens, -1))
    for mask in feed_masks[:0:-1]:
        keep, sent = halves(feed_moved, "seq", mask, feed_masks.index(mask))
        feed_moved = jnp.stack([keep, swap(sent, "seq", mask)], axis=feed_masks.index(mask))
        feed_moved = feed_moved.reshape(feed_moved.shape[: feed_masks.index(mask)] + (-1, tokens, feed_moved.shape[-1]))
    feed_keep, feed_sent = halves(feed_moved, "seq", feed_masks[0], 0)
    dgated, output_sent, feed_sent = together(dgated, output_sent, feed_sent)
    feed_other = swap(feed_sent, "seq", feed_masks[0])
    output_other = swap(output_sent, *narrow_stages[0][:2])

    dgated = dgated[:, :head_cols]
    gate_act, gate_slope = gelu_parts(gate_pre[:, :head_cols])[:2]
    dmixed = pad_columns(dgated * gate_act, tiles_of(heads))
    dgate = dgated * mixed[:, :head_cols] * gate_slope
    backward = functools.partial(chain_backward, resets, counts, cols, bias, dmixed, gain, shift, saved)
    part_a, kept = backward(part=(5, 8))

    part_a, kept, down_other, output_other, feed_other, dgate = together(part_a, kept, down_other, output_other, feed_other, dgate)
    dboth_row = jnp.stack([feed_keep, feed_other]).reshape(span, -1)
    feed_cols = dboth_row.shape[1]
    gate_part = t_dot(normed_row, dgate)
    feed = row_blocks(jnp.concatenate([t_dot(second_row, dboth_row), gate_part], axis=1))
    dnormed_gate = dot_t(dgate, own_gate[:, :head_cols])
    feed_stages = row_stages()
    feed_keep, feed_sent = halves(feed, *feed_stages[0])
    narrow = jnp.concatenate([down_keep + down_other, output_keep + output_other], axis=-2)
    narrow_keep, narrow_sent = halves(narrow, *narrow_stages[1])
    kept, feed_sent, narrow_sent, dnormed_gate = together(kept, feed_sent, narrow_sent, dnormed_gate)
    feed_other = swap(feed_sent, *feed_stages[0][:2])
    narrow_other = swap(narrow_sent, *narrow_stages[1][:2])
    part_b, kept = backward(part=(2, 5), before=kept)
    part_b, hidden, middle = together(part_b, hidden, middle)
    layer_output = middle + dot(hidden, down_weight)

    part_b, kept, narrow_other, feed_other = together(part_b, kept, narrow_other, feed_other)
    feed_keep, feed_sent = halves(feed_keep + feed_other, *feed_stages[1])
    narrow_keep, narrow_sent = halves(narrow_keep + narrow_other, *narrow_stages[2])
    kept, feed_sent, narrow_sent = together(kept, feed_sent, narrow_sent)
    feed_other = swap(feed_sent, *feed_stages[1][:2])
    narrow_other = swap(narrow_sent, *narrow_stages[2][:2])
    part_c, kept = backward(part=(0, 2), before=kept)

    part_c, kept, narrow_other, feed_other = together(part_c, kept, narrow_other, feed_other)
    feed = run_stages(feed_keep + feed_other, feed_stages[2:])
    narrow = run_stages(narrow_keep + narrow_other, narrow_stages[3:])
    seq_masks = bits_of("seq")[:-1]
    narrow = jnp.stack(jnp.split(narrow, n // 2, axis=1)).reshape((2,) * len(seq_masks) + (narrow.shape[0], -1))
    narrow = run_stages(narrow, [("seq", mask, seq_masks.index(mask)) for mask in reversed(seq_masks)])
    down_weight_grad, output_weight_grad = narrow[: ff // n_rows], narrow[ff // n_rows :]
    feed_weight_grad, gate_weight_grad = feed[:, :feed_cols], feed[:, feed_cols:]

    dcols = jnp.concatenate([part_c, part_b, part_a])
    triple_part = t_dot(normed_row, dcols)
    triple_blocks = row_blocks(triple_part)
    triple_sum = run_stages(triple_blocks, row_stages())
    dcols, triple_part = together(dcols, triple_part)
    dnormed = dot_t(dcols, own_mixer) + dnormed_gate
    dnormed = dnormed.reshape((2,) * len(bits_of("seq")) + (tokens, width))
    seq_order = [("seq", mask, bits_of("seq").index(mask)) for mask in reversed(bits_of("seq"))]
    dnormed = run_stages(dnormed, seq_order[:-1])
    dnormed_keep, dnormed_sent = halves(dnormed, *seq_order[-1])

    rate_tile = dcols[:, 3 * head_cols - rate_lane :][:, :LANES]
    rate_part = t_dot(rate_tile, normed_row)[rate_lane : rate_lane + heads]
    mixer_gain_part = jnp.sum(triple_part * own_mixer, axis=1)
    mixer_gain_part = (mixer_gain_part + jnp.sum(gate_part * own_gate[:, :head_cols], axis=1)) / mixer_gain
    gw1, gb1, gw2, gb2, ggain, gshift = kept[4:]
    lane_sums = jnp.sum(rate_tile, axis=0)[rate_lane : rate_lane + heads]
    narrow_rows = jnp.concatenate(
        [gb2[:, 0, :HEAD], jnp.sum(ggain, axis=1)[:, :HEAD], jnp.sum(gshift, axis=1)[:, :HEAD], lane_sums[:, None]], axis=1
    )
    pieces = [
        gw1.reshape(-1, INNER),
        gw2.reshape(-1, INNER),
        gb1[:, 0],
        pad_columns(narrow_rows, INNER),
        rate_part.reshape(-1, INNER),
        jnp.stack([mixer_gain_part, feed_gain_part]).reshape(-1, INNER),
    ]
    lengths = [piece.shape[0] for piece in pieces]
    rest = jnp.concatenate(pieces[2:])
    rest = jnp.pad(rest, ((0, -sum(lengths) % (n_rows * 8)), (0, 0)))
    small = jnp.concatenate(pieces[:2] + [rest])
    small, dnormed_sent = together(small, dnormed_sent)
    dnormed_other = swap(dnormed_sent, *seq_order[-1][:2])
    small = run_stages(row_blocks(small), row_stages())
    small = gather(small, "rows")
    small, dnormed_other = together(small, dnormed_other)
    small = gather(small, "seq").reshape(n, -1, INNER)
    starts = [sum(lengths[:at]) for at in range(len(lengths))]
    small = [small[:, start : start + length] for start, length in zip(starts, lengths)]
    first_weight_grad = small[0].reshape(n * heads, HEAD, INNER)[:HEADS]
    second_weight_grad = small[1].reshape(n * heads, HEAD, INNER)[:HEADS].transpose(0, 2, 1)
    first_bias_grad = small[2].reshape(n * heads, INNER)[:HEADS]
    narrow_rows = small[3].reshape(n * heads, INNER)[:HEADS]
    second_bias_grad, inner_gain_grad, inner_shift_grad = (narrow_rows[:, HEAD * at : HEAD * (at + 1)] for at in range(3))
    rate_bias_grad = narrow_rows[:, 3 * HEAD]
    rate_weight_grad = small[4].reshape(n * heads, width)[:HEADS].T
    gains = jnp.sum(small[5], axis=0).reshape(2, width)

    dxhat = (dnormed_keep + dnormed_other) * mixer_gain
    input_grad = dmiddle + inv * (dxhat - xhat * jnp.mean(dxhat * xhat, axis=-1, keepdims=True))

    triple_every = gather(triple_sum, "seq")
    share = 3 * width // n
    if n * heads == HEADS and share % head_cols == 0:
        blocks = []
        for at in range(share // head_cols):
            block = me * (share // head_cols) + at
            columns = lax.dynamic_slice(triple_every, (block % n, 0, block // n * head_cols), (1, triple_every.shape[1], head_cols))
            blocks.append(columns[0])
        triple_weight_grad = jnp.concatenate(blocks, axis=1)
    else:
        every = triple_every[:, :, : 3 * head_cols].reshape(n, -1, 3, head_cols).transpose(1, 2, 0, 3)
        every = every.reshape(every.shape[0], 3, -1)[:, :, :width].reshape(every.shape[0], 3 * width)
        triple_weight_grad = lax.dynamic_slice_in_dim(every, me * share, share, 1)
    if n * heads != HEADS:
        every = gather(gate_weight_grad, "seq").transpose(1, 0, 2)
        every = every.reshape(every.shape[0], -1)[:, :width]
        gate_weight_grad = lax.dynamic_slice_in_dim(every, me * (width // n), width // n, 1)

    return (
        layer_output[None],
        input_grad[None],
        gains[0],
        triple_weight_grad,
        rate_weight_grad,
        rate_bias_grad,
        first_weight_grad,
        first_bias_grad,
        second_weight_grad,
        second_bias_grad,
        inner_gain_grad,
        inner_shift_grad,
        gate_weight_grad,
        output_weight_grad,
        gains[1],
        feed_weight_grad,
        down_weight_grad,
    )


def solution(mesh):
    tokens = P("rows", "seq", None)
    shard = P("rows", "seq")
    in_specs = (tokens, P("rows", None), tokens) + (P(),) * 15
    out_specs = (tokens, tokens, P(), shard) + (P(),) * 8 + (shard, shard, P(), shard, shard)
    return jax.shard_map(local, mesh=mesh, in_specs=in_specs, out_specs=out_specs, check_vma=False)
```
